32 devices in a mesh: lat: 4 (over x, core), lon: 8 (over z, y).
Axes of the slice: x: 2, y: 2, z: 4, core: 2. Of those that a mesh axis runs over, the one named last changes fastest.
Arguments:
- queries: bfloat16 [64, 128, 1536], P('lat', 'lon'), may hold values from -12 to 12
- key_tokens: bfloat16 [64, 128, 1536], P('lat', 'lon'), may hold values from -4 to 4
- value_tokens: bfloat16 [64, 128, 1536], P('lat', 'lon'), may hold values from -6 to 6
- block_lists: int32 [8, 8, 8], P('lat', 'lon'), may hold values from 0 to 9, as said below
- band_rows: int32 [4, 128], P('lat', 'lon'), may hold values from 0 to 255, as said below
Outputs:
- attended: bfloat16 [64, 128, 1536], P('lat', 'lon')
The draws below stay inside these ranges and needn't reach their ends.
Inputs may be any that keep to these rules, and one draw needn't show every extreme that they name: `block_lists`: entry 0 of the list of query block b of a tile is its own block, 4 + b; the other entries are distinct candidate numbers, also distinct from entry 0. `band_rows`: the 16 token numbers of each tile are distinct.
All inputs are finite; a program needn't handle non-finite values.
Results may differ from the reference program's by a relative error of at most 0.0047.
Values may be sent and summed in bfloat16 or wider, within the bound.
A program may use at most 128 MiB of HBM per device.

```python
import jax
import jax.numpy as jnp
from jax import lax

H = 24
HD = 64
D = 1536
BR = 8
BW = 16
BS = 128
LT = 2
NB = 8
PR = 16
CAND = 10
ROWS = 64
COLS = 128
N_LAT = 4
N_LON = 8


def to_grid(blocked):
    split = blocked.reshape(N_LAT, LT, N_LON, BR, BW, D).transpose(0, 1, 3, 2, 4, 5)
    return split.reshape(ROWS, COLS, D)


def draw_key_tokens(key, part):
    own_key = jax.random.fold_in(key, 21)
    base_draw = jnp.clip(jax.random.normal(own_key, (N_LAT, LT, N_LON, BS, D), jnp.float32), -4.0, 4.0)
    return to_grid(base_draw).astype(jnp.bfloat16)


def draw_queries(key, part):
    own_key = jax.random.fold_in(key, 31)
    base_draw = jnp.clip(jax.random.normal(own_key, (N_LAT, LT, N_LON, BS, D), jnp.float32), -4.0, 4.0)
    return to_grid(base_draw).astype(jnp.bfloat16)


def draw_block_lists(key, part):
    own_key = jax.random.fold_in(key, 41)
    block_rows = LT * N_LAT
    ranks = jax.random.randint(own_key, (block_rows, N_LON, CAND), 0, 2 ** 16) * CAND + jnp.arange(CAND)[None, None, :]
    own_block = 2 * LT + jnp.arange(block_rows) % LT
    is_own = jnp.arange(CAND)[None, None, :] == own_block[:, None, None]
    ranks = jnp.where(is_own, -1, ranks)
    order = jnp.argsort(ranks, axis=-1)
    return order[:, :, :NB].astype(jnp.int32)


def draw_band_rows(key, part):
    own_key = jax.random.fold_in(key, 51)
    tile_size = LT * BS
    ranks = jax.random.randint(own_key, (N_LAT, N_LON, tile_size), 0, 2 ** 16) * tile_size + jnp.arange(tile_size)[None, None, :]
    order = jnp.argsort(ranks, axis=-1)
    return order[:, :, :PR].reshape(N_LAT, N_LON * PR).astype(jnp.int32)


def shard_levels(key, dims, cuts, least, largest):
    loudness, own = 1.0, jax.random.fold_in(key, 6)
    for position, parts in cuts:
        steps = jnp.exp(jax.random.uniform(jax.random.fold_in(own, position), (parts,), jnp.float32, least / len(cuts), largest / len(cuts)))
        loudness = loudness * jnp.repeat(steps, dims[position] // parts).reshape([-1 if axis == position else 1 for axis in range(len(dims))])
    return loudness


def bell_draw(stream_key, dims, width, limit, cuts=(), kind=jnp.bfloat16):
    entries = width * jax.random.normal(stream_key, dims, jnp.float32)
    if cuts:
        entries = entries * shard_levels(stream_key, dims, cuts, -0.22, 0.18)
    return jnp.clip(entries, -limit, limit).astype(kind)


def setup_inputs(seed: int = 0) -> dict:
    streams_of = jax.random.split(jax.random.key(seed), 6)
    return {
        "queries": draw_queries(jax.random.fold_in(streams_of[5], 71), 0),
        "key_tokens": draw_key_tokens(jax.random.fold_in(streams_of[5], 71), 0),
        "value_tokens": bell_draw(streams_of[2], (ROWS, COLS, D), 1.0, 6.0, ((0, 4), (1, 8))),
        "block_lists": draw_block_lists(jax.random.fold_in(streams_of[5], 71), 0),
        "band_rows": draw_band_rows(jax.random.fold_in(streams_of[5], 71), 0),
    }


def block_attention(q_rows, key_set, value_set, live_mask):
    count = q_rows.shape[0]
    q_heads = q_rows.reshape(count, H, HD).astype(jnp.float32)
    k_heads = key_set.reshape(key_set.shape[0], H, HD).astype(jnp.float32)
    v_heads = value_set.reshape(value_set.shape[0], H, HD).astype(jnp.float32)
    scores = jnp.einsum("qhd,khd->hqk", q_heads, k_heads) * (HD ** -0.5)
    scores = jnp.where(live_mask[None, None, :], scores, -jnp.inf)
    row_max = jnp.max(scores, axis=-1, keepdims=True)
    exp_scores = jnp.exp(scores - row_max)
    totals = jnp.sum(exp_scores, axis=-1)
    weights = exp_scores.astype(jnp.bfloat16)
    mixture = jnp.einsum("hqk,khd->qhd", weights.astype(jnp.float32), v_heads)
    mixture = mixture / jnp.transpose(totals)[:, :, None]
    return mixture.reshape(count, H * HD).astype(jnp.bfloat16)


def take_rows(tile, picks):
    return tile[picks]


def reference(queries, key_tokens, value_tokens, block_lists, band_rows):
    def tiles(source):
        grid = source.reshape(N_LAT, LT * BR, N_LON, BW, D).transpose(0, 2, 1, 3, 4)
        return grid.reshape(N_LAT, N_LON, LT, BS, D)

    q_tiles = tiles(queries)
    k_tiles = tiles(key_tokens)
    v_tiles = tiles(value_tokens)
    band_pick = band_rows.reshape(N_LAT, N_LON, PR)
    take_all = jax.vmap(jax.vmap(take_rows))
    band_keys = take_all(k_tiles.reshape(N_LAT, N_LON, LT * BS, D), band_pick).reshape(N_LAT, N_LON * PR, D)
    band_values = take_all(v_tiles.reshape(N_LAT, N_LON, LT * BS, D), band_pick).reshape(N_LAT, N_LON * PR, D)
    list_grid = block_lists.reshape(N_LAT, LT, N_LON, NB).transpose(0, 2, 1, 3)

    def device(dev_index):
        lat_at = dev_index // N_LON
        lon_at = dev_index % N_LON
        beside_all = (lon_at + jnp.arange(-2, 3, dtype=jnp.int32)) % N_LON
        cand_keys = k_tiles[lat_at, beside_all].reshape(CAND, BS, D)
        cand_values = v_tiles[lat_at, beside_all].reshape(CAND, BS, D)
        is_polar = (lat_at == 0) | (lat_at == N_LAT - 1)
        live_mask = jnp.concatenate([jnp.ones((NB * BS,), jnp.bool_), jnp.full((N_LON * PR,), is_polar)])

        def one_block(inputs):
            q_rows, listed = inputs
            key_set = jnp.concatenate([cand_keys[listed].reshape(NB * BS, D), band_keys[lat_at]], 0)
            value_set = jnp.concatenate([cand_values[listed].reshape(NB * BS, D), band_values[lat_at]], 0)
            return block_attention(q_rows, key_set, value_set, live_mask)

        return lax.map(one_block, (q_tiles[lat_at, lon_at], list_grid[lat_at, lon_at]))

    results = lax.map(device, jnp.arange(N_LAT * N_LON, dtype=jnp.int32))
    grid = results.reshape(N_LAT, N_LON, LT * BR, BW, D).transpose(0, 2, 1, 3, 4)
    return grid.reshape(ROWS, COLS, D)
```

```python
import functools

import jax
import jax.numpy as jnp
from jax import lax
from jax.experimental import pallas as pl
from jax.experimental.pallas import tpu as pltpu
from jax.sharding import PartitionSpec as P

HD = 64
BR = 8
BW = 16
PAIR = 2 * HD
MASKED = -1e30
MESH = pl.DeviceIdType.MESH


def kernel(
    n, n_lat, tile, picks,
    q_ref, k_ref, v_ref, lists_ref, rows_ref,
    out_ref,
    kv, staged, bias, send_sem, recv_sem, band_send, band_recv,
):
    groups = kv.shape[0]
    near = 5 * tile
    full = near + n * picks
    block = tile // 2
    me = lax.axis_index("lon")
    lat = lax.axis_index("lat")
    polar = (lat == 0) | (lat == n_lat - 1)
    odd = lax.rem(me, 2)
    partner = me + 1 - 2 * odd
    east = lax.rem(me + 2, n)
    west = lax.rem(me + n - 2, n)

    barrier = pltpu.get_barrier_semaphore()

    def greet(step, carry):
        pl.semaphore_signal(
            barrier, inc=1, device_id={"lon": lax.rem(me + step, n)}, device_id_type=MESH
        )
        return carry

    lax.fori_loop(1, n, greet, 0)

    for g in range(groups):
        columns = slice(g * PAIR, (g + 1) * PAIR)
        kv[g, 0, 2 * tile:3 * tile, :] = k_ref[:, columns]
        kv[g, 1, 2 * tile:3 * tile, :] = v_ref[:, columns]

    candidate = lax.broadcasted_iota(jnp.int32, (1, full), 1) // block
    for b in range(2):
        listed = candidate >= 10
        for slot in range(lists_ref.shape[2]):
            listed = listed | (candidate == lists_ref[b, 0, slot])
        bias[b:b + 1, :] = jnp.where(listed, 0.0, MASKED)

    @pl.when(polar)
    def _():
        row = lax.broadcasted_iota(jnp.int32, (picks, tile), 0)
        token = lax.broadcasted_iota(jnp.int32, (picks, tile), 1)
        hot = jnp.zeros((picks, tile), jnp.float32)
        for i in range(picks):
            hot = jnp.where((row == i) & (token == rows_ref[0, i]), 1.0, hot)
        hot = hot.astype(jnp.bfloat16)
        for which, ref in enumerate((k_ref, v_ref)):
            picked = jnp.dot(hot, ref[...], preferred_element_type=jnp.float32).astype(jnp.bfloat16)
            for g in range(groups):
                staged[g, which] = picked[:, g * PAIR:(g + 1) * PAIR]

    pl.semaphore_wait(barrier, n - 1)

    def tile_rows(t):
        return pl.ds(pl.multiple_of(t * tile, tile), tile)

    def own_copy(kind, g):
        target, t = ((east, 0), (west, 4), (partner, 1 + 2 * odd))[kind]
        return pltpu.make_async_remote_copy(
            src_ref=kv.at[g, :, tile_rows(2)],
            dst_ref=kv.at[g, :, tile_rows(t)],
            send_sem=send_sem.at[kind, g],
            recv_sem=recv_sem.at[kind, g],
            device_id={"lon": target},
            device_id_type=MESH,
        )

    def relay_copy(g):
        return pltpu.make_async_remote_copy(
            src_ref=kv.at[g, :, tile_rows(4 - 4 * odd)],
            dst_ref=kv.at[g, :, tile_rows(3 - 2 * odd)],
            send_sem=send_sem.at[3, g],
            recv_sem=recv_sem.at[3, g],
            device_id={"lon": partner},
            device_id_type=MESH,
        )

    def band_rows_of(j):
        return pl.ds(pl.multiple_of(near + j * picks, picks), picks)

    def band_copy(step):
        return pltpu.make_async_remote_copy(
            src_ref=staged,
            dst_ref=kv.at[:, :, band_rows_of(me)],
            send_sem=band_send.at[step],
            recv_sem=band_recv.at[step],
            device_id={"lon": lax.rem(me + step, n)},
            device_id_type=MESH,
        )

    def band_arrival(step):
        return pltpu.make_async_remote_copy(
            src_ref=staged,
            dst_ref=kv.at[:, :, band_rows_of(lax.rem(me + n - step, n))],
            send_sem=band_send.at[step],
            recv_sem=band_recv.at[step],
            device_id={"lon": lax.rem(me + step, n)},
            device_id_type=MESH,
        )

    def arrival(kind, t, g):
        return pltpu.make_async_remote_copy(
            src_ref=kv.at[g, :, tile_rows(2)],
            dst_ref=kv.at[g, :, tile_rows(t)],
            send_sem=send_sem.at[0, g],
            recv_sem=recv_sem.at[kind, g],
            device_id={"lon": partner},
            device_id_type=MESH,
        )

    @pl.when(polar)
    def _():
        def send(step, carry):
            band_copy(step).start()
            return carry

        lax.fori_loop(1, n, send, 0)
        for g in range(groups):
            kv[g, :, band_rows_of(me), :] = staged[g]

    def send_own(g, carry):
        for kind in range(3):
            own_copy(kind, g).start()
        return carry

    lax.fori_loop(0, groups, send_own, 0)

    def relay(g):
        arrival(1 - odd, 4 - 4 * odd, g).wait_recv()
        relay_copy(g).start()

    def attend(g, rows):
        columns = pl.ds(pl.multiple_of(g * PAIR, PAIR), PAIR)
        q = q_ref[:, columns] * jnp.bfloat16(HD ** -0.5)
        keys = kv[g, 0, 0:rows, :]
        values = jnp.concatenate(
            [kv[g, 1, 0:rows, :], jnp.ones((rows, PAIR), jnp.bfloat16)], axis=1
        )
        first = lax.broadcasted_iota(jnp.int32, (tile, PAIR), 1) < HD
        results = []
        for head in range(2):
            mine = first if head == 0 else ~first
            q_head = jnp.where(mine, q, jnp.zeros_like(q))
            scores = lax.dot_general(
                q_head, keys, (((1,), (1,)), ((), ())), preferred_element_type=jnp.float32
            )
            scores = scores.reshape(2, block, rows) + bias[:, 0:rows][:, None, :]
            scores = scores.reshape(tile, rows)
            row_max = jnp.max(scores, axis=-1, keepdims=True)
            weights = jnp.exp(scores - row_max).astype(jnp.bfloat16)
            mixed = jnp.dot(weights, values, preferred_element_type=jnp.float32)
            results.append(mixed[:, :PAIR] / mixed[:, PAIR:])
        out_ref[:, columns] = jnp.where(first, results[0], results[1]).astype(out_ref.dtype)

    relay(0)

    def step(g, carry):
        @pl.when(g + 1 < groups)
        def _():
            relay(g + 1)

        arrival(odd, 4 * odd, g).wait_recv()
        arrival(2, 3 - 2 * odd, g).wait_recv()
        arrival(3, 1 + 2 * odd, g).wait_recv()

        @pl.when(polar)
        def _():
            @pl.when(g == 0)
            def _():
                def take(s, c):
                    band_arrival(s).wait_recv()
                    return c

                lax.fori_loop(1, n, take, 0)

            attend(g, full)

        @pl.when(jnp.logical_not(polar))
        def _():
            attend(g, near)

        return carry

    lax.fori_loop(0, groups, step, 0)

    def drain(g, carry):
        for kind in range(3):
            own_copy(kind, g).wait_send()
        relay_copy(g).wait_send()
        return carry

    lax.fori_loop(0, groups, drain, 0)

    @pl.when(polar)
    def _():
        def drain_band(s, c):
            band_copy(s).wait_send()
            return c

        lax.fori_loop(1, n, drain_band, 0)


def local(n, n_lat, queries, key_tokens, value_tokens, block_lists, band_rows):
    tile_lat, tile_lon, feature = queries.shape
    tile = tile_lat * tile_lon
    picks = band_rows.shape[1]
    groups = feature // PAIR
    full = 5 * tile + n * picks
    vmem = pl.BlockSpec(memory_space=pltpu.VMEM)
    smem = pl.BlockSpec(memory_space=pltpu.SMEM)
    out = pl.pallas_call(
        functools.partial(kernel, n, n_lat, tile, picks),
        out_shape=jax.ShapeDtypeStruct((tile, feature), queries.dtype),
        in_specs=[vmem, vmem, vmem, smem, smem],
        out_specs=vmem,
        scratch_shapes=[
            pltpu.VMEM((groups, 2, full, PAIR), jnp.bfloat16),
            pltpu.VMEM((groups, 2, picks, PAIR), jnp.bfloat16),
            pltpu.VMEM((2, full), jnp.float32),
            pltpu.SemaphoreType.DMA((4, groups)),
            pltpu.SemaphoreType.DMA((4, groups)),
            pltpu.SemaphoreType.DMA((n,)),
            pltpu.SemaphoreType.DMA((n,)),
        ],
        compiler_params=pltpu.CompilerParams(
            collective_id=0, has_side_effects=True, vmem_limit_bytes=56 * 1024 * 1024
        ),
    )(
        queries.reshape(tile, feature),
        key_tokens.reshape(tile, feature),
        value_tokens.reshape(tile, feature),
        block_lists,
        band_rows,
    )
    return out.reshape(tile_lat, tile_lon, feature)


def solution(mesh):
    return jax.shard_map(
        functools.partial(local, mesh.shape["lon"], mesh.shape["lat"]),
        mesh=mesh,
        in_specs=(
            P("lat", "lon", None),
            P("lat", "lon", None),
            P("lat", "lon", None),
            P("lat", "lon", None),
            P("lat", "lon"),
        ),
        out_specs=P("lat", "lon", None),
        check_vma=False,
    )
```

```python
import functools

import jax
import jax.numpy as jnp
from jax import lax
from jax.experimental import pallas as pl
from jax.experimental.pallas import tpu as pltpu
from jax.sharding import PartitionSpec as P

HD = 64
BR = 8
BW = 16
PAIR = 2 * HD
MASKED = -1e30
MESH = pl.DeviceIdType.MESH


def kernel(
    n, n_lat, tile, picks,
    q_ref, k_ref, v_ref, lists_ref, rows_ref,
    out_ref,
    kv, staged, selectors, bias, send_sem, recv_sem, far_send, far_recv, hot_send, hot_recv,
    half_send, half_recv,
):
    groups = kv.shape[0]
    near = 5 * tile
    full = near + n * picks
    block = tile // 2
    half = n // 2
    me = lax.axis_index("lon")
    lat = lax.axis_index("lat")
    polar = (lat == 0) | (lat == n_lat - 1)
    odd = lax.rem(me, 2)
    partner = me + 1 - 2 * odd
    east = lax.rem(me + 2, n)
    west = lax.rem(me + n - 2, n)

    barrier = pltpu.get_barrier_semaphore()

    def greet(peer):
        pl.semaphore_signal(barrier, inc=1, device_id={"lon": peer}, device_id_type=MESH)

    greet(partner)
    greet(east)
    greet(west)

    @pl.when(polar)
    def _():
        def greet_far(step, carry):
            greet(lax.rem(me + 2 * step, n))
            return carry

        lax.fori_loop(2, half - 1, greet_far, 0)

    for g in range(groups):
        columns = slice(g * PAIR, (g + 1) * PAIR)
        kv[g, 0, 2 * tile:3 * tile, :] = k_ref[:, columns]
        kv[g, 1, 2 * tile:3 * tile, :] = v_ref[:, columns]

    def band_rows_of(j):
        place = lax.rem(j, 2) * half + j // 2
        return pl.ds(pl.multiple_of(near + place * picks, picks), picks)

    candidate = lax.broadcasted_iota(jnp.int32, (1, full), 1) // block
    for b in range(2):
        listed = candidate >= 10
        for slot in range(lists_ref.shape[2]):
            listed = listed | (candidate == lists_ref[b, 0, slot])
        bias[b:b + 1, :] = jnp.where(listed, 0.0, MASKED)

    @pl.when(polar)
    def _():
        row = lax.broadcasted_iota(jnp.int32, (picks, tile), 0)
        token = lax.broadcasted_iota(jnp.int32, (picks, tile), 1)
        hot = jnp.zeros((picks, tile), jnp.float32)
        for i in range(picks):
            hot = jnp.where((row == i) & (token == rows_ref[0, i]), 1.0, hot)
        hot = hot.astype(jnp.bfloat16)
        selectors[1] = hot
        for which, ref in enumerate((k_ref, v_ref)):
            picked = jnp.dot(hot, ref[...], preferred_element_type=jnp.float32).astype(jnp.bfloat16)
            for g in range(groups):
                chunk = picked[:, g * PAIR:(g + 1) * PAIR]
                staged[g, which] = chunk
                kv[g, which, band_rows_of(me), :] = chunk

    pl.semaphore_wait(barrier, jnp.where(polar, half, 3))

    def tile_rows(t):
        return pl.ds(pl.multiple_of(t * tile, tile), tile)

    def own_copy(kind, g):
        target, t = ((east, 0), (west, 4), (partner, 1 + 2 * odd))[kind]
        return pltpu.make_async_remote_copy(
            src_ref=kv.at[g, :, tile_rows(2)],
            dst_ref=kv.at[g, :, tile_rows(t)],
            send_sem=send_sem.at[kind, g],
            recv_sem=recv_sem.at[kind, g],
            device_id={"lon": target},
            device_id_type=MESH,
        )

    def relay_copy(g):
        return pltpu.make_async_remote_copy(
            src_ref=kv.at[g, :, tile_rows(4 - 4 * odd)],
            dst_ref=kv.at[g, :, tile_rows(3 - 2 * odd)],
            send_sem=send_sem.at[3, g],
            recv_sem=recv_sem.at[3, g],
            device_id={"lon": partner},
            device_id_type=MESH,
        )

    def far_copy(step):
        return pltpu.make_async_remote_copy(
            src_ref=staged,
            dst_ref=kv.at[:, :, band_rows_of(me)],
            send_sem=far_send.at[step],
            recv_sem=far_recv.at[step],
            device_id={"lon": lax.rem(me + 2 * step, n)},
            device_id_type=MESH,
        )

    def far_arrival(step):
        return pltpu.make_async_remote_copy(
            src_ref=staged,
            dst_ref=kv.at[:, :, band_rows_of(lax.rem(me + n - 2 * step, n))],
            send_sem=far_send.at[step],
            recv_sem=far_recv.at[step],
            device_id={"lon": lax.rem(me + 2 * step, n)},
            device_id_type=MESH,
        )

    def hot_copy(way):
        return pltpu.make_async_remote_copy(
            src_ref=selectors.at[1],
            dst_ref=selectors.at[2 * way],
            send_sem=hot_send.at[way],
            recv_sem=hot_recv.at[way],
            device_id={"lon": (east, west)[way]},
            device_id_type=MESH,
        )

    def half_rows(parity):
        return pl.ds(pl.multiple_of(near + parity * (half * picks), half * picks), half * picks)

    def half_copy(g, parity):
        return pltpu.make_async_remote_copy(
            src_ref=kv.at[g, :, half_rows(parity)],
            dst_ref=kv.at[g, :, half_rows(parity)],
            send_sem=half_send.at[g],
            recv_sem=half_recv.at[g],
            device_id={"lon": partner},
            device_id_type=MESH,
        )

    def arrival(kind, t, g):
        return pltpu.make_async_remote_copy(
            src_ref=kv.at[g, :, tile_rows(2)],
            dst_ref=kv.at[g, :, tile_rows(t)],
            send_sem=send_sem.at[0, g],
            recv_sem=recv_sem.at[kind, g],
            device_id={"lon": partner},
            device_id_type=MESH,
        )

    @pl.when(polar)
    def _():
        hot_copy(0).start()
        hot_copy(1).start()

        def send(step, carry):
            far_copy(step).start()
            return carry

        lax.fori_loop(2, half - 1, send, 0)

    def send_own(g, carry):
        for kind in range(3):
            own_copy(kind, g).start()
        return carry

    lax.fori_loop(0, groups, send_own, 0)

    def relay(g):
        arrival(1 - odd, 4 - 4 * odd, g).wait_recv()
        relay_copy(g).start()
        arrival(odd, 4 * odd, g).wait_recv()

        @pl.when(polar)
        def _():
            for which in range(2):
                for way, peer in ((0, west), (2, east)):
                    rows = kv[g, which, 2 * way * tile:(2 * way + 1) * tile, :]
                    picked = jnp.dot(selectors[way], rows, preferred_element_type=jnp.float32)
                    kv[g, which, band_rows_of(peer), :] = picked.astype(jnp.bfloat16)
            half_copy(g, odd).start()

    def attend(g, rows):
        columns = pl.ds(pl.multiple_of(g * PAIR, PAIR), PAIR)
        q = q_ref[:, columns] * jnp.bfloat16(HD ** -0.5)
        keys = kv[g, 0, 0:rows, :]
        values = jnp.concatenate(
            [kv[g, 1, 0:rows, :], jnp.ones((rows, PAIR), jnp.bfloat16)], axis=1
        )
        first = lax.broadcasted_iota(jnp.int32, (tile, PAIR), 1) < HD
        results = []
        for head in range(2):
            mine = first if head == 0 else ~first
            q_head = jnp.where(mine, q, jnp.zeros_like(q))
            scores = lax.dot_general(
                q_head, keys, (((1,), (1,)), ((), ())), preferred_element_type=jnp.float32
            )
            scores = scores.reshape(2, block, rows) + bias[:, 0:rows][:, None, :]
            scores = scores.reshape(tile, rows)
            row_max = jnp.max(scores, axis=-1, keepdims=True)
            weights = jnp.exp(scores - row_max).astype(jnp.bfloat16)
            mixed = jnp.dot(weights, values, preferred_element_type=jnp.float32)
            results.append(mixed[:, :PAIR] / mixed[:, PAIR:])
        out_ref[:, columns] = jnp.where(first, results[0], results[1]).astype(out_ref.dtype)

    @pl.when(polar)
    def _():
        hot_copy(0).wait_recv()
        hot_copy(1).wait_recv()

        def take(s, c):
            far_arrival(s).wait_recv()
            return c

        lax.fori_loop(2, half - 1, take, 0)

    relay(0)

    def step(g, carry):
        @pl.when(g + 1 < groups)
        def _():
            relay(g + 1)

        arrival(2, 3 - 2 * odd, g).wait_recv()
        arrival(3, 1 + 2 * odd, g).wait_recv()

        @pl.when(polar)
        def _():
            half_copy(g, 1 - odd).wait_recv()
            attend(g, full)

        @pl.when(jnp.logical_not(polar))
        def _():
            attend(g, near)

        return carry

    lax.fori_loop(0, groups, step, 0)

    def drain(g, carry):
        for kind in range(3):
            own_copy(kind, g).wait_send()
        relay_copy(g).wait_send()
        return carry

    lax.fori_loop(0, groups, drain, 0)

    @pl.when(polar)
    def _():
        hot_copy(0).wait_send()
        hot_copy(1).wait_send()

        def drain_far(s, c):
            far_copy(s).wait_send()
            return c

        lax.fori_loop(2, half - 1, drain_far, 0)

        def drain_half(g, c):
            half_copy(g, odd).wait_send()
            return c

        lax.fori_loop(0, groups, drain_half, 0)


def local(n, n_lat, queries, key_tokens, value_tokens, block_lists, band_rows):
    tile_lat, tile_lon, feature = queries.shape
    tile = tile_lat * tile_lon
    picks = band_rows.shape[1]
    groups = feature // PAIR
    full = 5 * tile + n * picks
    vmem = pl.BlockSpec(memory_space=pltpu.VMEM)
    smem = pl.BlockSpec(memory_space=pltpu.SMEM)
    out = pl.pallas_call(
        functools.partial(kernel, n, n_lat, tile, picks),
        out_shape=jax.ShapeDtypeStruct((tile, feature), queries.dtype),
        in_specs=[vmem, vmem, vmem, smem, smem],
        out_specs=vmem,
        scratch_shapes=[
            pltpu.VMEM((groups, 2, full, PAIR), jnp.bfloat16),
            pltpu.VMEM((groups, 2, picks, PAIR), jnp.bfloat16),
            pltpu.VMEM((3, picks, tile), jnp.bfloat16),
            pltpu.VMEM((2, full), jnp.float32),
            pltpu.SemaphoreType.DMA((4, groups)),
            pltpu.SemaphoreType.DMA((4, groups)),
            pltpu.SemaphoreType.DMA((n // 2,)),
            pltpu.SemaphoreType.DMA((n // 2,)),
            pltpu.SemaphoreType.DMA((2,)),
            pltpu.SemaphoreType.DMA((2,)),
            pltpu.SemaphoreType.DMA((groups,)),
            pltpu.SemaphoreType.DMA((groups,)),
        ],
        compiler_params=pltpu.CompilerParams(
            collective_id=0, has_side_effects=True, vmem_limit_bytes=36 * 1024 * 1024
        ),
    )(
        queries.reshape(tile, feature),
        key_tokens.reshape(tile, feature),
        value_tokens.reshape(tile, feature),
        block_lists,
        band_rows,
    )
    return out.reshape(tile_lat, tile_lon, feature)


def solution(mesh):
    return jax.shard_map(
        functools.partial(local, mesh.shape["lon"], mesh.shape["lat"]),
        mesh=mesh,
        in_specs=(
            P("lat", "lon", None),
            P("lat", "lon", None),
            P("lat", "lon", None),
            P("lat", "lon", None),
            P("lat", "lon"),
        ),
        out_specs=P("lat", "lon", None),
        check_vma=False,
    )
```

```python
import functools

import jax
import jax.numpy as jnp
from jax import lax
from jax.experimental import pallas as pl
from jax.experimental.pallas import tpu as pltpu
from jax.sharding import PartitionSpec as P

HD = 64
BR = 8
BW = 16
PAIR = 2 * HD
MASKED = -1e30
MESH = pl.DeviceIdType.MESH


def kernel(
    n, n_lat, tile, picks,
    q_in, k_in, v_in, lists_ref, rows_ref,
    out_ref,
    q_ref, kv, staged, selectors, bias, send_sem, recv_sem, far_send, far_recv, hot_send, hot_recv,
    half_send, half_recv, load_sem, q_sem,
):
    groups = kv.shape[0]
    near = 5 * tile
    full = near + n * picks
    block = tile // 2
    half = n // 2
    early = 2
    me = lax.axis_index("lon")
    lat = lax.axis_index("lat")
    polar = (lat == 0) | (lat == n_lat - 1)
    odd = lax.rem(me, 2)
    partner = me + 1 - 2 * odd
    east = lax.rem(me + 2, n)
    west = lax.rem(me + n - 2, n)

    def load(g, which):
        columns = pl.ds(pl.multiple_of(g * PAIR, PAIR), PAIR)
        return pltpu.make_async_copy(
            (k_in, v_in)[which].at[:, columns],
            kv.at[g, which, pl.ds(2 * tile, tile)],
            load_sem.at[which, g],
        )

    for g in range(groups):
        load(g, 0).start()
        load(g, 1).start()
    q_load = pltpu.make_async_copy(q_in, q_ref, q_sem)
    q_load.start()

    barrier = pltpu.get_barrier_semaphore()

    def greet(peer):
        pl.semaphore_signal(barrier, inc=1, device_id={"lon": peer}, device_id_type=MESH)

    greet(partner)
    greet(east)
    greet(west)

    @pl.when(polar)
    def _():
        def greet_far(step, carry):
            greet(lax.rem(me + 2 * step, n))
            return carry

        lax.fori_loop(2, half - 1, greet_far, 0)

    def band_rows_of(j):
        place = lax.rem(j, 2) * half + j // 2
        return pl.ds(pl.multiple_of(near + place * picks, picks), picks)

    pl.semaphore_wait(barrier, jnp.where(polar, half, 3))

    def tile_rows(t):
        return pl.ds(pl.multiple_of(t * tile, tile), tile)

    def own_copy(kind, g):
        target, t = ((east, 0), (west, 4), (partner, 1 + 2 * odd))[kind]
        return pltpu.make_async_remote_copy(
            src_ref=kv.at[g, :, tile_rows(2)],
            dst_ref=kv.at[g, :, tile_rows(t)],
            send_sem=send_sem.at[kind, g],
            recv_sem=recv_sem.at[kind, g],
            device_id={"lon": target},
            device_id_type=MESH,
        )

    def relay_copy(g):
        return pltpu.make_async_remote_copy(
            src_ref=kv.at[g, :, tile_rows(4 - 4 * odd)],
            dst_ref=kv.at[g, :, tile_rows(3 - 2 * odd)],
            send_sem=send_sem.at[3, g],
            recv_sem=recv_sem.at[3, g],
            device_id={"lon": partner},
            device_id_type=MESH,
        )

    def far_copy(step):
        return pltpu.make_async_remote_copy(
            src_ref=staged,
            dst_ref=kv.at[:, :, band_rows_of(me)],
            send_sem=far_send.at[step],
            recv_sem=far_recv.at[step],
            device_id={"lon": lax.rem(me + 2 * step, n)},
            device_id_type=MESH,
        )

    def far_arrival(step):
        return pltpu.make_async_remote_copy(
            src_ref=staged,
            dst_ref=kv.at[:, :, band_rows_of(lax.rem(me + n - 2 * step, n))],
            send_sem=far_send.at[step],
            recv_sem=far_recv.at[step],
            device_id={"lon": lax.rem(me + 2 * step, n)},
            device_id_type=MESH,
        )

    def hot_copy(way):
        return pltpu.make_async_remote_copy(
            src_ref=selectors.at[1],
            dst_ref=selectors.at[2 * way],
            send_sem=hot_send.at[way],
            recv_sem=hot_recv.at[way],
            device_id={"lon": (east, west)[way]},
            device_id_type=MESH,
        )

    def half_rows(parity):
        return pl.ds(pl.multiple_of(near + parity * (half * picks), half * picks), half * picks)

    def half_copy(g, parity):
        return pltpu.make_async_remote_copy(
            src_ref=kv.at[g, :, half_rows(parity)],
            dst_ref=kv.at[g, :, half_rows(parity)],
            send_sem=half_send.at[g],
            recv_sem=half_recv.at[g],
            device_id={"lon": partner},
            device_id_type=MESH,
        )

    def arrival(kind, t, g):
        return pltpu.make_async_remote_copy(
            src_ref=kv.at[g, :, tile_rows(2)],
            dst_ref=kv.at[g, :, tile_rows(t)],
            send_sem=send_sem.at[0, g],
            recv_sem=recv_sem.at[kind, g],
            device_id={"lon": partner},
            device_id_type=MESH,
        )

    def send_own(g, carry):
        load(g, 0).wait()
        load(g, 1).wait()
        for kind in range(3):
            own_copy(kind, g).start()
        return carry

    lax.fori_loop(0, early, send_own, 0)

    @pl.when(polar)
    def _():
        row = lax.broadcasted_iota(jnp.int32, (picks, tile), 0)
        token = lax.broadcasted_iota(jnp.int32, (picks, tile), 1)
        hot = jnp.zeros((picks, tile), jnp.float32)
        for i in range(picks):
            hot = jnp.where((row == i) & (token == rows_ref[0, i]), 1.0, hot)
        selectors[1] = hot.astype(jnp.bfloat16)
        hot_copy(0).start()
        hot_copy(1).start()

    def await_load(g, carry):
        load(g, 0).wait()
        load(g, 1).wait()
        return carry

    lax.fori_loop(early, groups, await_load, 0)

    @pl.when(polar)
    def _():
        def pick_own(g, carry):
            for which in range(2):
                rows = kv[g, which, 2 * tile:3 * tile, :]
                picked = jnp.dot(selectors[1], rows, preferred_element_type=jnp.float32)
                staged[g, which] = picked.astype(jnp.bfloat16)
                kv[g, which, band_rows_of(me), :] = picked.astype(jnp.bfloat16)
            return carry

        lax.fori_loop(0, groups, pick_own, 0)

        def send(step, carry):
            far_copy(step).start()
            return carry

        lax.fori_loop(2, half - 1, send, 0)

    def send_rest(g, carry):
        for kind in range(3):
            own_copy(kind, g).start()
        return carry

    lax.fori_loop(early, groups, send_rest, 0)

    candidate = lax.broadcasted_iota(jnp.int32, (1, full), 1) // block
    for b in range(2):
        listed = candidate >= 10
        for slot in range(lists_ref.shape[2]):
            listed = listed | (candidate == lists_ref[b, 0, slot])
        bias[b:b + 1, :] = jnp.where(listed, 0.0, MASKED)

    q_load.wait()

    def relay(g):
        arrival(1 - odd, 4 - 4 * odd, g).wait_recv()
        relay_copy(g).start()
        arrival(odd, 4 * odd, g).wait_recv()

        @pl.when(polar)
        def _():
            for which in range(2):
                for way, peer in ((0, west), (2, east)):
                    rows = kv[g, which, 2 * way * tile:(2 * way + 1) * tile, :]
                    picked = jnp.dot(selectors[way], rows, preferred_element_type=jnp.float32)
                    kv[g, which, band_rows_of(peer), :] = picked.astype(jnp.bfloat16)
            half_copy(g, odd).start()

    def attend(g, rows):
        columns = pl.ds(pl.multiple_of(g * PAIR, PAIR), PAIR)
        q = q_ref[:, columns] * jnp.bfloat16(HD ** -0.5)
        keys = kv[g, 0, 0:rows, :]
        values = jnp.concatenate(
            [kv[g, 1, 0:rows, :], jnp.ones((rows, PAIR), jnp.bfloat16)], axis=1
        )
        first = lax.broadcasted_iota(jnp.int32, (tile, PAIR), 1) < HD
        results = []
        for head in range(2):
            mine = first if head == 0 else ~first
            q_head = jnp.where(mine, q, jnp.zeros_like(q))
            scores = lax.dot_general(
                q_head, keys, (((1,), (1,)), ((), ())), preferred_element_type=jnp.float32
            )
            scores = scores.reshape(2, block, rows) + bias[:, 0:rows][:, None, :]
            scores = scores.reshape(tile, rows)
            row_max = jnp.max(scores, axis=-1, keepdims=True)
            weights = jnp.exp(scores - row_max).astype(jnp.bfloat16)
            mixed = jnp.dot(weights, values, preferred_element_type=jnp.float32)
            results.append(mixed[:, :PAIR] / mixed[:, PAIR:])
        out_ref[:, columns] = jnp.where(first, results[0], results[1]).astype(out_ref.dtype)

    @pl.when(polar)
    def _():
        hot_copy(0).wait_recv()
        hot_copy(1).wait_recv()

        def take(s, c):
            far_arrival(s).wait_recv()
            return c

        lax.fori_loop(2, half - 1, take, 0)

    relay(0)

    def step(g, carry):
        @pl.when(g + 1 < groups)
        def _():
            relay(g + 1)

        arrival(2, 3 - 2 * odd, g).wait_recv()
        arrival(3, 1 + 2 * odd, g).wait_recv()

        @pl.when(polar)
        def _():
            half_copy(g, 1 - odd).wait_recv()
            attend(g, full)

        @pl.when(jnp.logical_not(polar))
        def _():
            attend(g, near)

        return carry

    lax.fori_loop(0, groups, step, 0)

    def drain(g, carry):
        for kind in range(3):
            own_copy(kind, g).wait_send()
        relay_copy(g).wait_send()
        return carry

    lax.fori_loop(0, groups, drain, 0)

    @pl.when(polar)
    def _():
        hot_copy(0).wait_send()
        hot_copy(1).wait_send()

        def drain_far(s, c):
            far_copy(s).wait_send()
            return c

        lax.fori_loop(2, half - 1, drain_far, 0)

        def drain_half(g, c):
            half_copy(g, odd).wait_send()
            return c

        lax.fori_loop(0, groups, drain_half, 0)


def local(n, n_lat, queries, key_tokens, value_tokens, block_lists, band_rows):
    tile_lat, tile_lon, feature = queries.shape
    tile = tile_lat * tile_lon
    picks = band_rows.shape[1]
    groups = feature // PAIR
    full = 5 * tile + n * picks
    vmem = pl.BlockSpec(memory_space=pltpu.VMEM)
    hbm = pl.BlockSpec(memory_space=pltpu.HBM)
    smem = pl.BlockSpec(memory_space=pltpu.SMEM)
    out = pl.pallas_call(
        functools.partial(kernel, n, n_lat, tile, picks),
        out_shape=jax.ShapeDtypeStruct((tile, feature), queries.dtype),
        in_specs=[hbm, hbm, hbm, smem, smem],
        out_specs=vmem,
        scratch_shapes=[
            pltpu.VMEM((tile, feature), queries.dtype),
            pltpu.VMEM((groups, 2, full, PAIR), jnp.bfloat16),
            pltpu.VMEM((groups, 2, picks, PAIR), jnp.bfloat16),
            pltpu.VMEM((3, picks, tile), jnp.bfloat16),
            pltpu.VMEM((2, full), jnp.float32),
            pltpu.SemaphoreType.DMA((4, groups)),
            pltpu.SemaphoreType.DMA((4, groups)),
            pltpu.SemaphoreType.DMA((n // 2,)),
            pltpu.SemaphoreType.DMA((n // 2,)),
            pltpu.SemaphoreType.DMA((2,)),
            pltpu.SemaphoreType.DMA((2,)),
            pltpu.SemaphoreType.DMA((groups,)),
            pltpu.SemaphoreType.DMA((groups,)),
            pltpu.SemaphoreType.DMA((2, groups)),
            pltpu.SemaphoreType.DMA,
        ],
        compiler_params=pltpu.CompilerParams(
            collective_id=0, has_side_effects=True, vmem_limit_bytes=56 * 1024 * 1024
        ),
    )(
        queries.reshape(tile, feature),
        key_tokens.reshape(tile, feature),
        value_tokens.reshape(tile, feature),
        block_lists,
        band_rows,
    )
    return out.reshape(tile_lat, tile_lon, feature)


def solution(mesh):
    return jax.shard_map(
        functools.partial(local, mesh.shape["lon"], mesh.shape["lat"]),
        mesh=mesh,
        in_specs=(
            P("lat", "lon", None),
            P("lat", "lon", None),
            P("lat", "lon", None),
            P("lat", "lon", None),
            P("lat", "lon"),
        ),
        out_specs=P("lat", "lon", None),
        check_vma=False,
    )
```

```python
import functools

import jax
import jax.numpy as jnp
from jax import lax
from jax.experimental import pallas as pl
from jax.experimental.pallas import tpu as pltpu
from jax.sharding import PartitionSpec as P

HD = 64
BR = 8
BW = 16
PAIR = 2 * HD
MASKED = -1e30
MESH = pl.DeviceIdType.MESH


def kernel(
    n, n_lat, tile, picks,
    q_in, k_in, v_in, lists_ref, rows_ref,
    out_ref,
    q_ref, kv, staged, selectors, bias, send_sem, recv_sem, far_send, far_recv, hot_send, hot_recv,
    half_send, half_recv, load_sem, q_sem,
):
    groups = kv.shape[0]
    near = 5 * tile
    full = near + n * picks
    block = tile // 2
    half = n // 2
    early = 2
    window = 4
    me = lax.axis_index("lon")
    lat = lax.axis_index("lat")
    polar = (lat == 0) | (lat == n_lat - 1)
    odd = lax.rem(me, 2)
    partner = me + 1 - 2 * odd
    east = lax.rem(me + 2, n)
    west = lax.rem(me + n - 2, n)

    def load(g, which):
        columns = pl.ds(pl.multiple_of(g * PAIR, PAIR), PAIR)
        return pltpu.make_async_copy(
            (k_in, v_in)[which].at[:, columns],
            kv.at[g, which, pl.ds(2 * tile, tile)],
            load_sem.at[which, g],
        )

    for g in range(groups):
        load(g, 0).start()
        load(g, 1).start()
    q_load = pltpu.make_async_copy(q_in, q_ref, q_sem)
    q_load.start()

    barrier = pltpu.get_barrier_semaphore()

    def greet(peer):
        pl.semaphore_signal(barrier, inc=1, device_id={"lon": peer}, device_id_type=MESH)

    greet(partner)
    greet(east)
    greet(west)

    @pl.when(polar)
    def _():
        def greet_far(step, carry):
            greet(lax.rem(me + 2 * step, n))
            return carry

        lax.fori_loop(2, half - 1, greet_far, 0)

    def band_rows_of(j):
        place = lax.rem(j, 2) * half + j // 2
        return pl.ds(pl.multiple_of(near + place * picks, picks), picks)

    pl.semaphore_wait(barrier, jnp.where(polar, half, 3))

    def tile_rows(t):
        return pl.ds(pl.multiple_of(t * tile, tile), tile)

    def own_copy(kind, g):
        target, t = ((east, 0), (west, 4), (partner, 1 + 2 * odd))[kind]
        return pltpu.make_async_remote_copy(
            src_ref=kv.at[g, :, tile_rows(2)],
            dst_ref=kv.at[g, :, tile_rows(t)],
            send_sem=send_sem.at[kind, g],
            recv_sem=recv_sem.at[kind, g],
            device_id={"lon": target},
            device_id_type=MESH,
        )

    def relay_copy(g):
        return pltpu.make_async_remote_copy(
            src_ref=kv.at[g, :, tile_rows(4 - 4 * odd)],
            dst_ref=kv.at[g, :, tile_rows(3 - 2 * odd)],
            send_sem=send_sem.at[3, g],
            recv_sem=recv_sem.at[3, g],
            device_id={"lon": partner},
            device_id_type=MESH,
        )

    def far_copy(step):
        return pltpu.make_async_remote_copy(
            src_ref=staged,
            dst_ref=kv.at[:, :, band_rows_of(me)],
            send_sem=far_send.at[step],
            recv_sem=far_recv.at[step],
            device_id={"lon": lax.rem(me + 2 * step, n)},
            device_id_type=MESH,
        )

    def far_arrival(step):
        return pltpu.make_async_remote_copy(
            src_ref=staged,
            dst_ref=kv.at[:, :, band_rows_of(lax.rem(me + n - 2 * step, n))],
            send_sem=far_send.at[step],
            recv_sem=far_recv.at[step],
            device_id={"lon": lax.rem(me + 2 * step, n)},
            device_id_type=MESH,
        )

    def hot_copy(way):
        return pltpu.make_async_remote_copy(
            src_ref=selectors.at[1],
            dst_ref=selectors.at[2 * way],
            send_sem=hot_send.at[way],
            recv_sem=hot_recv.at[way],
            device_id={"lon": (east, west)[way]},
            device_id_type=MESH,
        )

    def half_rows(parity):
        return pl.ds(pl.multiple_of(near + parity * (half * picks), half * picks), half * picks)

    def half_copy(g, parity):
        return pltpu.make_async_remote_copy(
            src_ref=kv.at[g, :, half_rows(parity)],
            dst_ref=kv.at[g, :, half_rows(parity)],
            send_sem=half_send.at[g],
            recv_sem=half_recv.at[g],
            device_id={"lon": partner},
            device_id_type=MESH,
        )

    def arrival(kind, t, g):
        return pltpu.make_async_remote_copy(
            src_ref=kv.at[g, :, tile_rows(2)],
            dst_ref=kv.at[g, :, tile_rows(t)],
            send_sem=send_sem.at[0, g],
            recv_sem=recv_sem.at[kind, g],
            device_id={"lon": partner},
            device_id_type=MESH,
        )

    def send_own(g, carry):
        load(g, 0).wait()
        load(g, 1).wait()
        for kind in range(3):
            own_copy(kind, g).start()
        return carry

    lax.fori_loop(0, early, send_own, 0)

    @pl.when(polar)
    def _():
        row = lax.broadcasted_iota(jnp.int32, (picks, tile), 0)
        token = lax.broadcasted_iota(jnp.int32, (picks, tile), 1)
        hot = jnp.zeros((picks, tile), jnp.float32)
        for i in range(picks):
            hot = jnp.where((row == i) & (token == rows_ref[0, i]), 1.0, hot)
        selectors[1] = hot.astype(jnp.bfloat16)
        hot_copy(0).start()
        hot_copy(1).start()

    def await_load(g, carry):
        load(g, 0).wait()
        load(g, 1).wait()
        return carry

    lax.fori_loop(early, groups, await_load, 0)

    @pl.when(polar)
    def _():
        def pick_own(g, carry):
            for which in range(2):
                rows = kv[g, which, 2 * tile:3 * tile, :]
                picked = jnp.dot(selectors[1], rows, preferred_element_type=jnp.float32)
                staged[g, which] = picked.astype(jnp.bfloat16)
                kv[g, which, band_rows_of(me), :] = picked.astype(jnp.bfloat16)
            return carry

        lax.fori_loop(0, groups, pick_own, 0)

        def send(step, carry):
            far_copy(step).start()
            return carry

        lax.fori_loop(2, half - 1, send, 0)

    def send_rest(g, carry):
        for kind in range(3):
            own_copy(kind, g).start()
        return carry

    lax.fori_loop(early, window, send_rest, 0)

    candidate = lax.broadcasted_iota(jnp.int32, (1, full), 1) // block
    for b in range(2):
        listed = candidate >= 10
        for slot in range(lists_ref.shape[2]):
            listed = listed | (candidate == lists_ref[b, 0, slot])
        bias[b:b + 1, :] = jnp.where(listed, 0.0, MASKED)

    q_load.wait()

    def relay(g):
        arrival(1 - odd, 4 - 4 * odd, g).wait_recv()
        relay_copy(g).start()
        arrival(odd, 4 * odd, g).wait_recv()

        @pl.when(polar)
        def _():
            for which in range(2):
                for way, peer in ((0, west), (2, east)):
                    rows = kv[g, which, 2 * way * tile:(2 * way + 1) * tile, :]
                    picked = jnp.dot(selectors[way], rows, preferred_element_type=jnp.float32)
                    kv[g, which, band_rows_of(peer), :] = picked.astype(jnp.bfloat16)
            half_copy(g, odd).start()

    def attend(g, rows):
        columns = pl.ds(pl.multiple_of(g * PAIR, PAIR), PAIR)
        q = q_ref[:, columns] * jnp.bfloat16(HD ** -0.5)
        keys = kv[g, 0, 0:rows, :]
        values = jnp.concatenate(
            [kv[g, 1, 0:rows, :], jnp.ones((rows, PAIR), jnp.bfloat16)], axis=1
        )
        first = lax.broadcasted_iota(jnp.int32, (tile, PAIR), 1) < HD
        results = []
        for head in range(2):
            mine = first if head == 0 else ~first
            q_head = jnp.where(mine, q, jnp.zeros_like(q))
            scores = lax.dot_general(
                q_head, keys, (((1,), (1,)), ((), ())), preferred_element_type=jnp.float32
            )
            scores = scores.reshape(2, block, rows) + bias[:, 0:rows][:, None, :]
            scores = scores.reshape(tile, rows)
            row_max = jnp.max(scores, axis=-1, keepdims=True)
            weights = jnp.exp(scores - row_max).astype(jnp.bfloat16)
            mixed = jnp.dot(weights, values, preferred_element_type=jnp.float32)
            results.append(mixed[:, :PAIR] / mixed[:, PAIR:])
        out_ref[:, columns] = jnp.where(first, results[0], results[1]).astype(out_ref.dtype)

    @pl.when(polar)
    def _():
        hot_copy(0).wait_recv()
        hot_copy(1).wait_recv()

        def take(s, c):
            far_arrival(s).wait_recv()
            return c

        lax.fori_loop(2, half - 1, take, 0)

    relay(0)

    def step(g, carry):
        @pl.when(g + 1 < groups)
        def _():
            relay(g + 1)

        @pl.when(g + window < groups)
        def _():
            for kind in range(3):
                own_copy(kind, g).wait_send()
            for kind in range(3):
                own_copy(kind, g + window).start()

        arrival(2, 3 - 2 * odd, g).wait_recv()
        arrival(3, 1 + 2 * odd, g).wait_recv()

        @pl.when(polar)
        def _():
            half_copy(g, 1 - odd).wait_recv()
            attend(g, full)

        @pl.when(jnp.logical_not(polar))
        def _():
            attend(g, near)

        return carry

    lax.fori_loop(0, groups, step, 0)

    def drain(g, carry):
        @pl.when(g + window >= groups)
        def _():
            for kind in range(3):
                own_copy(kind, g).wait_send()

        relay_copy(g).wait_send()
        return carry

    lax.fori_loop(0, groups, drain, 0)

    @pl.when(polar)
    def _():
        hot_copy(0).wait_send()
        hot_copy(1).wait_send()

        def drain_far(s, c):
            far_copy(s).wait_send()
            return c

        lax.fori_loop(2, half - 1, drain_far, 0)

        def drain_half(g, c):
            half_copy(g, odd).wait_send()
            return c

        lax.fori_loop(0, groups, drain_half, 0)


def local(n, n_lat, queries, key_tokens, value_tokens, block_lists, band_rows):
    tile_lat, tile_lon, feature = queries.shape
    tile = tile_lat * tile_lon
    picks = band_rows.shape[1]
    groups = feature // PAIR
    full = 5 * tile + n * picks
    vmem = pl.BlockSpec(memory_space=pltpu.VMEM)
    hbm = pl.BlockSpec(memory_space=pltpu.HBM)
    smem = pl.BlockSpec(memory_space=pltpu.SMEM)
    out = pl.pallas_call(
        functools.partial(kernel, n, n_lat, tile, picks),
        out_shape=jax.ShapeDtypeStruct((tile, feature), queries.dtype),
        in_specs=[hbm, hbm, hbm, smem, smem],
        out_specs=vmem,
        scratch_shapes=[
            pltpu.VMEM((tile, feature), queries.dtype),
            pltpu.VMEM((groups, 2, full, PAIR), jnp.bfloat16),
            pltpu.VMEM((groups, 2, picks, PAIR), jnp.bfloat16),
            pltpu.VMEM((3, picks, tile), jnp.bfloat16),
            pltpu.VMEM((2, full), jnp.float32),
            pltpu.SemaphoreType.DMA((4, groups)),
            pltpu.SemaphoreType.DMA((4, groups)),
            pltpu.SemaphoreType.DMA((n // 2,)),
            pltpu.SemaphoreType.DMA((n // 2,)),
            pltpu.SemaphoreType.DMA((2,)),
            pltpu.SemaphoreType.DMA((2,)),
            pltpu.SemaphoreType.DMA((groups,)),
            pltpu.SemaphoreType.DMA((groups,)),
            pltpu.SemaphoreType.DMA((2, groups)),
            pltpu.SemaphoreType.DMA,
        ],
        compiler_params=pltpu.CompilerParams(
            collective_id=0, has_side_effects=True, vmem_limit_bytes=53 * 1024 * 1024
        ),
    )(
        queries.reshape(tile, feature),
        key_tokens.reshape(tile, feature),
        value_tokens.reshape(tile, feature),
        block_lists,
        band_rows,
    )
    return out.reshape(tile_lat, tile_lon, feature)


def solution(mesh):
    return jax.shard_map(
        functools.partial(local, mesh.shape["lon"], mesh.shape["lat"]),
        mesh=mesh,
        in_specs=(
            P("lat", "lon", None),
            P("lat", "lon", None),
            P("lat", "lon", None),
            P("lat", "lon", None),
            P("lat", "lon"),
        ),
        out_specs=P("lat", "lon", None),
        check_vma=False,
    )
```

```python
import functools

import jax
import jax.numpy as jnp
from jax import lax
from jax.experimental import pallas as pl
from jax.experimental.pallas import tpu as pltpu
from jax.sharding import PartitionSpec as P

HD = 64
BR = 8
BW = 16
PAIR = 2 * HD
MASKED = -1e30
MESH = pl.DeviceIdType.MESH


def kernel(
    n, n_lat, tile, picks,
    q_in, k_in, v_in, lists_ref, rows_ref,
    out_ref,
    q_ref, kv, staged, selectors, bias, send_sem, recv_sem, far_send, far_recv, hot_send, hot_recv,
    outer_send, outer_recv, beyond_send, beyond_recv, load_sem, q_sem,
):
    groups = kv.shape[0]
    near = 5 * tile
    full = near + n * picks
    block = tile // 2
    half = n // 2
    early = 2
    window = 4
    me = lax.axis_index("lon")
    lat = lax.axis_index("lat")
    polar = (lat == 0) | (lat == n_lat - 1)
    odd = lax.rem(me, 2)
    partner = me + 1 - 2 * odd
    east = lax.rem(me + 2, n)
    west = lax.rem(me + n - 2, n)

    def load(g, which):
        columns = pl.ds(pl.multiple_of(g * PAIR, PAIR), PAIR)
        return pltpu.make_async_copy(
            (k_in, v_in)[which].at[:, columns],
            kv.at[g, which, pl.ds(2 * tile, tile)],
            load_sem.at[which, g],
        )

    barrier = pltpu.get_barrier_semaphore()

    def greet(peer):
        pl.semaphore_signal(barrier, inc=1, device_id={"lon": peer}, device_id_type=MESH)

    greet(partner)
    greet(east)
    greet(west)

    @pl.when(polar)
    def _():
        def greet_far(step, carry):
            greet(lax.rem(me + 2 * step, n))
            return carry

        lax.fori_loop(2, half - 1, greet_far, 0)

    for g in range(groups):
        load(g, 0).start()
        load(g, 1).start()
    q_load = pltpu.make_async_copy(q_in, q_ref, q_sem)
    q_load.start()

    def band_rows_of(j):
        place = lax.rem(j, 2) * half + j // 2
        return pl.ds(pl.multiple_of(near + place * picks, picks), picks)

    pl.semaphore_wait(barrier, jnp.where(polar, half, 3))

    def tile_rows(t):
        return pl.ds(pl.multiple_of(t * tile, tile), tile)

    def own_copy(kind, g):
        target, t = ((east, 0), (west, 4), (partner, 1 + 2 * odd))[kind]
        return pltpu.make_async_remote_copy(
            src_ref=kv.at[g, :, tile_rows(2)],
            dst_ref=kv.at[g, :, tile_rows(t)],
            send_sem=send_sem.at[kind, g],
            recv_sem=recv_sem.at[kind, g],
            device_id={"lon": target},
            device_id_type=MESH,
        )

    def relay_copy(g):
        return pltpu.make_async_remote_copy(
            src_ref=kv.at[g, :, tile_rows(4 - 4 * odd)],
            dst_ref=kv.at[g, :, tile_rows(3 - 2 * odd)],
            send_sem=send_sem.at[3, g],
            recv_sem=recv_sem.at[3, g],
            device_id={"lon": partner},
            device_id_type=MESH,
        )

    def far_copy(step):
        return pltpu.make_async_remote_copy(
            src_ref=staged,
            dst_ref=kv.at[:, :, band_rows_of(me)],
            send_sem=far_send.at[step],
            recv_sem=far_recv.at[step],
            device_id={"lon": lax.rem(me + 2 * step, n)},
            device_id_type=MESH,
        )

    def far_arrival(step):
        return pltpu.make_async_remote_copy(
            src_ref=staged,
            dst_ref=kv.at[:, :, band_rows_of(lax.rem(me + n - 2 * step, n))],
            send_sem=far_send.at[step],
            recv_sem=far_recv.at[step],
            device_id={"lon": lax.rem(me + 2 * step, n)},
            device_id_type=MESH,
        )

    def hot_copy(kind):
        target, t = ((east, 0), (west, 4), (partner, 1 + 2 * odd), (partner, 3 - 2 * odd))[kind]
        return pltpu.make_async_remote_copy(
            src_ref=selectors.at[2 if kind < 3 else 4 - 4 * odd],
            dst_ref=selectors.at[t],
            send_sem=hot_send.at[kind],
            recv_sem=hot_recv.at[kind],
            device_id={"lon": target},
            device_id_type=MESH,
        )

    def hot_arrival(kind):
        t = (0, 4, 3 - 2 * odd, 1 + 2 * odd)[kind]
        return pltpu.make_async_remote_copy(
            src_ref=selectors.at[2],
            dst_ref=selectors.at[t],
            send_sem=hot_send.at[kind],
            recv_sem=hot_recv.at[kind],
            device_id={"lon": partner},
            device_id_type=MESH,
        )

    def outer_rows(j):
        return band_rows_of(lax.rem(j + n + 4 * lax.rem(j, 2) - 2, n))

    def outer_copy(g, j):
        return pltpu.make_async_remote_copy(
            src_ref=kv.at[g, :, outer_rows(j)],
            dst_ref=kv.at[g, :, outer_rows(j)],
            send_sem=outer_send.at[g],
            recv_sem=outer_recv.at[g],
            device_id={"lon": partner},
            device_id_type=MESH,
        )

    def beyond_copy(step, j):
        rows = band_rows_of(lax.rem(j + n - 2 * step, n))
        return pltpu.make_async_remote_copy(
            src_ref=kv.at[:, :, rows],
            dst_ref=kv.at[:, :, rows],
            send_sem=beyond_send.at[step],
            recv_sem=beyond_recv.at[step],
            device_id={"lon": partner},
            device_id_type=MESH,
        )

    def pick(g, t, peer):
        for which in range(2):
            rows = kv[g, which, tile_rows(t), :]
            picked = jnp.dot(selectors[t], rows, preferred_element_type=jnp.float32)
            kv[g, which, band_rows_of(peer), :] = picked.astype(jnp.bfloat16)

    def arrival(kind, t, g):
        return pltpu.make_async_remote_copy(
            src_ref=kv.at[g, :, tile_rows(2)],
            dst_ref=kv.at[g, :, tile_rows(t)],
            send_sem=send_sem.at[0, g],
            recv_sem=recv_sem.at[kind, g],
            device_id={"lon": partner},
            device_id_type=MESH,
        )

    def send_own(g, carry):
        load(g, 0).wait()
        load(g, 1).wait()
        for kind in range(3):
            own_copy(kind, g).start()
        return carry

    lax.fori_loop(0, early, send_own, 0)

    @pl.when(polar)
    def _():
        row = lax.broadcasted_iota(jnp.int32, (picks, tile), 0)
        token = lax.broadcasted_iota(jnp.int32, (picks, tile), 1)
        hot = jnp.zeros((picks, tile), jnp.float32)
        for i in range(picks):
            hot = jnp.where((row == i) & (token == rows_ref[0, i]), 1.0, hot)
        selectors[2] = hot.astype(jnp.bfloat16)
        for kind in range(3):
            hot_copy(kind).start()

    def await_load(g, carry):
        load(g, 0).wait()
        load(g, 1).wait()
        return carry

    lax.fori_loop(early, groups, await_load, 0)

    @pl.when(polar)
    def _():
        def pick_own(g, carry):
            for which in range(2):
                rows = kv[g, which, 2 * tile:3 * tile, :]
                picked = jnp.dot(selectors[2], rows, preferred_element_type=jnp.float32)
                staged[g, which] = picked.astype(jnp.bfloat16)
                kv[g, which, band_rows_of(me), :] = picked.astype(jnp.bfloat16)
            return carry

        lax.fori_loop(0, groups, pick_own, 0)

        def send(step, carry):
            far_copy(step).start()
            return carry

        lax.fori_loop(2, half - 1, send, 0)

    def send_rest(g, carry):
        for kind in range(3):
            own_copy(kind, g).start()
        return carry

    lax.fori_loop(early, window, send_rest, 0)

    candidate = lax.broadcasted_iota(jnp.int32, (1, full), 1) // block
    for b in range(2):
        listed = candidate >= 10
        for slot in range(lists_ref.shape[2]):
            listed = listed | (candidate == lists_ref[b, 0, slot])
        bias[b:b + 1, :] = jnp.where(listed, 0.0, MASKED)

    q_load.wait()

    def relay(g):
        arrival(1 - odd, 4 - 4 * odd, g).wait_recv()
        relay_copy(g).start()
        arrival(odd, 4 * odd, g).wait_recv()

        @pl.when(polar)
        def _():
            pick(g, 0, west)
            pick(g, 4, east)
            outer_copy(g, me).start()

    def attend(g, rows):
        columns = pl.ds(pl.multiple_of(g * PAIR, PAIR), PAIR)
        q = q_ref[:, columns] * jnp.bfloat16(HD ** -0.5)
        keys = kv[g, 0, 0:rows, :]
        values = jnp.concatenate(
            [kv[g, 1, 0:rows, :], jnp.ones((rows, PAIR), jnp.bfloat16)], axis=1
        )
        first = lax.broadcasted_iota(jnp.int32, (tile, PAIR), 1) < HD
        results = []
        for head in range(2):
            mine = first if head == 0 else ~first
            q_head = jnp.where(mine, q, jnp.zeros_like(q))
            scores = lax.dot_general(
                q_head, keys, (((1,), (1,)), ((), ())), preferred_element_type=jnp.float32
            )
            scores = scores.reshape(2, block, rows) + bias[:, 0:rows][:, None, :]
            scores = scores.reshape(tile, rows)
            row_max = jnp.max(scores, axis=-1, keepdims=True)
            weights = jnp.exp(scores - row_max).astype(jnp.bfloat16)
            mixed = jnp.dot(weights, values, preferred_element_type=jnp.float32)
            results.append(mixed[:, :PAIR] / mixed[:, PAIR:])
        out_ref[:, columns] = jnp.where(first, results[0], results[1]).astype(out_ref.dtype)

    @pl.when(polar)
    def _():
        for kind in range(2):
            hot_arrival(kind).wait_recv()
        hot_copy(3).start()

        def take(s, c):
            far_arrival(s).wait_recv()
            beyond_copy(s, me).start()
            return c

        lax.fori_loop(2, half - 1, take, 0)

    relay(0)

    def step(g, carry):
        @pl.when(g + 1 < groups)
        def _():
            relay(g + 1)

        @pl.when(g + window < groups)
        def _():
            for kind in range(3):
                own_copy(kind, g).wait_send()
            for kind in range(3):
                own_copy(kind, g + window).start()

        arrival(2, 3 - 2 * odd, g).wait_recv()
        arrival(3, 1 + 2 * odd, g).wait_recv()

        @pl.when(polar)
        def _():
            @pl.when(g == 0)
            def _():
                hot_arrival(2).wait_recv()
                hot_arrival(3).wait_recv()

                def take_beyond(s, c):
                    beyond_copy(s, partner).wait_recv()
                    return c

                lax.fori_loop(2, half - 1, take_beyond, 0)

            pick(g, 3 - 2 * odd, partner)
            pick(g, 1 + 2 * odd, lax.rem(me + n - 1 + 2 * odd, n))
            outer_copy(g, partner).wait_recv()
            attend(g, full)

        @pl.when(jnp.logical_not(polar))
        def _():
            attend(g, near)

        return carry

    lax.fori_loop(0, groups, step, 0)

    def drain(g, carry):
        @pl.when(g + window >= groups)
        def _():
            for kind in range(3):
                own_copy(kind, g).wait_send()

        relay_copy(g).wait_send()
        return carry

    lax.fori_loop(0, groups, drain, 0)

    @pl.when(polar)
    def _():
        for kind in range(4):
            hot_copy(kind).wait_send()

        def drain_far(s, c):
            far_copy(s).wait_send()
            beyond_copy(s, me).wait_send()
            return c

        lax.fori_loop(2, half - 1, drain_far, 0)

        def drain_outer(g, c):
            outer_copy(g, me).wait_send()
            return c

        lax.fori_loop(0, groups, drain_outer, 0)


def local(n, n_lat, queries, key_tokens, value_tokens, block_lists, band_rows):
    tile_lat, tile_lon, feature = queries.shape
    tile = tile_lat * tile_lon
    picks = band_rows.shape[1]
    groups = feature // PAIR
    full = 5 * tile + n * picks
    vmem = pl.BlockSpec(memory_space=pltpu.VMEM)
    hbm = pl.BlockSpec(memory_space=pltpu.HBM)
    smem = pl.BlockSpec(memory_space=pltpu.SMEM)
    out = pl.pallas_call(
        functools.partial(kernel, n, n_lat, tile, picks),
        out_shape=jax.ShapeDtypeStruct((tile, feature), queries.dtype),
        in_specs=[hbm, hbm, hbm, smem, smem],
        out_specs=vmem,
        scratch_shapes=[
            pltpu.VMEM((tile, feature), queries.dtype),
            pltpu.VMEM((groups, 2, full, PAIR), jnp.bfloat16),
            pltpu.VMEM((groups, 2, picks, PAIR), jnp.bfloat16),
            pltpu.VMEM((5, picks, tile), jnp.bfloat16),
            pltpu.VMEM((2, full), jnp.float32),
            pltpu.SemaphoreType.DMA((4, groups)),
            pltpu.SemaphoreType.DMA((4, groups)),
            pltpu.SemaphoreType.DMA((n // 2,)),
            pltpu.SemaphoreType.DMA((n // 2,)),
            pltpu.SemaphoreType.DMA((4,)),
            pltpu.SemaphoreType.DMA((4,)),
            pltpu.SemaphoreType.DMA((groups,)),
            pltpu.SemaphoreType.DMA((groups,)),
            pltpu.SemaphoreType.DMA((n // 2,)),
            pltpu.SemaphoreType.DMA((n // 2,)),
            pltpu.SemaphoreType.DMA((2, groups)),
            pltpu.SemaphoreType.DMA,
        ],
        compiler_params=pltpu.CompilerParams(
            collective_id=0, has_side_effects=True, vmem_limit_bytes=53 * 1024 * 1024
        ),
    )(
        queries.reshape(tile, feature),
        key_tokens.reshape(tile, feature),
        value_tokens.reshape(tile, feature),
        block_lists,
        band_rows,
    )
    return out.reshape(tile_lat, tile_lon, feature)


def solution(mesh):
    return jax.shard_map(
        functools.partial(local, mesh.shape["lon"], mesh.shape["lat"]),
        mesh=mesh,
        in_specs=(
            P("lat", "lon", None),
            P("lat", "lon", None),
            P("lat", "lon", None),
            P("lat", "lon", None),
            P("lat", "lon"),
        ),
        out_specs=P("lat", "lon", None),
        check_vma=False,
    )
```

```python
import functools

import jax
import jax.numpy as jnp
from jax import lax
from jax.experimental import pallas as pl
from jax.experimental.pallas import tpu as pltpu
from jax.sharding import PartitionSpec as P

HD = 64
BR = 8
BW = 16
PAIR = 2 * HD
MASKED = -1e30
MESH = pl.DeviceIdType.MESH


def kernel(
    n, n_lat, tile, picks,
    q_in, k_in, v_in, lists_ref, rows_ref,
    out_ref,
    q_ref, kv, staged, selectors, bias, send_sem, recv_sem, far_send, far_recv, hot_send, hot_recv,
    outer_send, outer_recv, beyond_send, beyond_recv, load_sem, q_sem,
):
    groups = kv.shape[0]
    near = 5 * tile
    full = near + n * picks
    block = tile // 2
    half = n // 2
    early = 2
    me = lax.axis_index("lon")
    lat = lax.axis_index("lat")
    polar = (lat == 0) | (lat == n_lat - 1)
    window = jnp.where(polar, 8, 2)
    odd = lax.rem(me, 2)
    partner = me + 1 - 2 * odd
    east = lax.rem(me + 2, n)
    west = lax.rem(me + n - 2, n)

    def load(g, which):
        columns = pl.ds(pl.multiple_of(g * PAIR, PAIR), PAIR)
        return pltpu.make_async_copy(
            (k_in, v_in)[which].at[:, columns],
            kv.at[g, which, pl.ds(2 * tile, tile)],
            load_sem.at[which, g],
        )

    barrier = pltpu.get_barrier_semaphore()

    def greet(peer):
        pl.semaphore_signal(barrier, inc=1, device_id={"lon": peer}, device_id_type=MESH)

    greet(partner)
    greet(east)
    greet(west)

    @pl.when(polar)
    def _():
        def greet_far(step, carry):
            greet(lax.rem(me + 2 * step, n))
            return carry

        lax.fori_loop(2, half - 1, greet_far, 0)

    for g in range(groups):
        load(g, 0).start()
        load(g, 1).start()
    q_load = pltpu.make_async_copy(q_in, q_ref, q_sem)
    q_load.start()

    def band_rows_of(j):
        place = lax.rem(j, 2) * half + j // 2
        return pl.ds(pl.multiple_of(near + place * picks, picks), picks)

    pl.semaphore_wait(barrier, jnp.where(polar, half, 3))

    def tile_rows(t):
        return pl.ds(pl.multiple_of(t * tile, tile), tile)

    def own_copy(kind, g):
        target, t = ((east, 0), (west, 4), (partner, 1 + 2 * odd))[kind]
        return pltpu.make_async_remote_copy(
            src_ref=kv.at[g, :, tile_rows(2)],
            dst_ref=kv.at[g, :, tile_rows(t)],
            send_sem=send_sem.at[kind, g],
            recv_sem=recv_sem.at[kind, g],
            device_id={"lon": target},
            device_id_type=MESH,
        )

    def relay_copy(g):
        return pltpu.make_async_remote_copy(
            src_ref=kv.at[g, :, tile_rows(4 - 4 * odd)],
            dst_ref=kv.at[g, :, tile_rows(3 - 2 * odd)],
            send_sem=send_sem.at[3, g],
            recv_sem=recv_sem.at[3, g],
            device_id={"lon": partner},
            device_id_type=MESH,
        )

    def far_copy(step):
        return pltpu.make_async_remote_copy(
            src_ref=staged,
            dst_ref=kv.at[:, :, band_rows_of(me)],
            send_sem=far_send.at[step],
            recv_sem=far_recv.at[step],
            device_id={"lon": lax.rem(me + 2 * step, n)},
            device_id_type=MESH,
        )

    def far_arrival(step):
        return pltpu.make_async_remote_copy(
            src_ref=staged,
            dst_ref=kv.at[:, :, band_rows_of(lax.rem(me + n - 2 * step, n))],
            send_sem=far_send.at[step],
            recv_sem=far_recv.at[step],
            device_id={"lon": lax.rem(me + 2 * step, n)},
            device_id_type=MESH,
        )

    def hot_copy(kind):
        target, t = ((east, 0), (west, 4), (partner, 1 + 2 * odd), (partner, 3 - 2 * odd))[kind]
        return pltpu.make_async_remote_copy(
            src_ref=selectors.at[2 if kind < 3 else 4 - 4 * odd],
            dst_ref=selectors.at[t],
            send_sem=hot_send.at[kind],
            recv_sem=hot_recv.at[kind],
            device_id={"lon": target},
            device_id_type=MESH,
        )

    def hot_arrival(kind):
        t = (0, 4, 3 - 2 * odd, 1 + 2 * odd)[kind]
        return pltpu.make_async_remote_copy(
            src_ref=selectors.at[2],
            dst_ref=selectors.at[t],
            send_sem=hot_send.at[kind],
            recv_sem=hot_recv.at[kind],
            device_id={"lon": partner},
            device_id_type=MESH,
        )

    def outer_rows(j):
        return band_rows_of(lax.rem(j + n + 4 * lax.rem(j, 2) - 2, n))

    def outer_copy(g, j):
        return pltpu.make_async_remote_copy(
            src_ref=kv.at[g, :, outer_rows(j)],
            dst_ref=kv.at[g, :, outer_rows(j)],
            send_sem=outer_send.at[g],
            recv_sem=outer_recv.at[g],
            device_id={"lon": partner},
            device_id_type=MESH,
        )

    def beyond_copy(step, j):
        rows = band_rows_of(lax.rem(j + n - 2 * step, n))
        return pltpu.make_async_remote_copy(
            src_ref=kv.at[:, :, rows],
            dst_ref=kv.at[:, :, rows],
            send_sem=beyond_send.at[step],
            recv_sem=beyond_recv.at[step],
            device_id={"lon": partner},
            device_id_type=MESH,
        )

    def pick(g, t, peer):
        for which in range(2):
            rows = kv[g, which, tile_rows(t), :]
            picked = jnp.dot(selectors[t], rows, preferred_element_type=jnp.float32)
            kv[g, which, band_rows_of(peer), :] = picked.astype(jnp.bfloat16)

    def arrival(kind, t, g):
        return pltpu.make_async_remote_copy(
            src_ref=kv.at[g, :, tile_rows(2)],
            dst_ref=kv.at[g, :, tile_rows(t)],
            send_sem=send_sem.at[0, g],
            recv_sem=recv_sem.at[kind, g],
            device_id={"lon": partner},
            device_id_type=MESH,
        )

    def send_own(g, carry):
        load(g, 0).wait()
        load(g, 1).wait()
        for kind in range(3):
            own_copy(kind, g).start()
        return carry

    lax.fori_loop(0, early, send_own, 0)

    @pl.when(polar)
    def _():
        row = lax.broadcasted_iota(jnp.int32, (picks, tile), 0)
        token = lax.broadcasted_iota(jnp.int32, (picks, tile), 1)
        hot = jnp.zeros((picks, tile), jnp.float32)
        for i in range(picks):
            hot = jnp.where((row == i) & (token == rows_ref[0, i]), 1.0, hot)
        selectors[2] = hot.astype(jnp.bfloat16)
        for kind in range(3):
            hot_copy(kind).start()

    def await_load(g, carry):
        load(g, 0).wait()
        load(g, 1).wait()
        return carry

    lax.fori_loop(early, groups, await_load, 0)

    @pl.when(polar)
    def _():
        def pick_own(g, carry):
            for which in range(2):
                rows = kv[g, which, 2 * tile:3 * tile, :]
                picked = jnp.dot(selectors[2], rows, preferred_element_type=jnp.float32)
                staged[g, which] = picked.astype(jnp.bfloat16)
                kv[g, which, band_rows_of(me), :] = picked.astype(jnp.bfloat16)
            return carry

        lax.fori_loop(0, groups, pick_own, 0)

        def send(step, carry):
            far_copy(step).start()
            return carry

        lax.fori_loop(2, half - 1, send, 0)

    def send_rest(g, carry):
        for kind in range(3):
            own_copy(kind, g).start()
        return carry

    lax.fori_loop(early, window, send_rest, 0)

    candidate = lax.broadcasted_iota(jnp.int32, (1, full), 1) // block
    for b in range(2):
        listed = candidate >= 10
        for slot in range(lists_ref.shape[2]):
            listed = listed | (candidate == lists_ref[b, 0, slot])
        bias[b:b + 1, :] = jnp.where(listed, 0.0, MASKED)

    q_load.wait()

    def relay(g):
        arrival(1 - odd, 4 - 4 * odd, g).wait_recv()
        relay_copy(g).start()
        arrival(odd, 4 * odd, g).wait_recv()

        @pl.when(polar)
        def _():
            pick(g, 0, west)
            pick(g, 4, east)
            outer_copy(g, me).start()

    def attend(g, rows):
        columns = pl.ds(pl.multiple_of(g * PAIR, PAIR), PAIR)
        q = q_ref[:, columns] * jnp.bfloat16(HD ** -0.5)
        keys = kv[g, 0, 0:rows, :]
        values = jnp.concatenate(
            [kv[g, 1, 0:rows, :], jnp.ones((rows, PAIR), jnp.bfloat16)], axis=1
        )
        first = lax.broadcasted_iota(jnp.int32, (tile, PAIR), 1) < HD
        results = []
        for head in range(2):
            mine = first if head == 0 else ~first
            q_head = jnp.where(mine, q, jnp.zeros_like(q))
            scores = lax.dot_general(
                q_head, keys, (((1,), (1,)), ((), ())), preferred_element_type=jnp.float32
            )
            scores = scores.reshape(2, block, rows) + bias[:, 0:rows][:, None, :]
            scores = scores.reshape(tile, rows)
            row_max = jnp.max(scores, axis=-1, keepdims=True)
            weights = jnp.exp(scores - row_max).astype(jnp.bfloat16)
            mixed = jnp.dot(weights, values, preferred_element_type=jnp.float32)
            results.append(mixed[:, :PAIR] / mixed[:, PAIR:])
        out_ref[:, columns] = jnp.where(first, results[0], results[1]).astype(out_ref.dtype)

    @pl.when(polar)
    def _():
        for kind in range(2):
            hot_arrival(kind).wait_recv()
        hot_copy(3).start()

        def take(s, c):
            far_arrival(s).wait_recv()
            beyond_copy(s, me).start()
            return c

        lax.fori_loop(2, half - 1, take, 0)

    relay(0)

    def step(g, carry):
        @pl.when(g + 1 < groups)
        def _():
            relay(g + 1)

        @pl.when(g + window < groups)
        def _():
            for kind in range(3):
                own_copy(kind, g).wait_send()
            for kind in range(3):
                own_copy(kind, g + window).start()

        arrival(2, 3 - 2 * odd, g).wait_recv()
        arrival(3, 1 + 2 * odd, g).wait_recv()

        @pl.when(polar)
        def _():
            @pl.when(g == 0)
            def _():
                hot_arrival(2).wait_recv()
                hot_arrival(3).wait_recv()

                def take_beyond(s, c):
                    beyond_copy(s, partner).wait_recv()
                    return c

                lax.fori_loop(2, half - 1, take_beyond, 0)

            pick(g, 3 - 2 * odd, partner)
            pick(g, 1 + 2 * odd, lax.rem(me + n - 1 + 2 * odd, n))
            outer_copy(g, partner).wait_recv()
            attend(g, full)

        @pl.when(jnp.logical_not(polar))
        def _():
            attend(g, near)

        return carry

    lax.fori_loop(0, groups, step, 0)

    def drain(g, carry):
        @pl.when(g + window >= groups)
        def _():
            for kind in range(3):
                own_copy(kind, g).wait_send()

        relay_copy(g).wait_send()
        return carry

    lax.fori_loop(0, groups, drain, 0)

    @pl.when(polar)
    def _():
        for kind in range(4):
            hot_copy(kind).wait_send()

        def drain_far(s, c):
            far_copy(s).wait_send()
            beyond_copy(s, me).wait_send()
            return c

        lax.fori_loop(2, half - 1, drain_far, 0)

        def drain_outer(g, c):
            outer_copy(g, me).wait_send()
            return c

        lax.fori_loop(0, groups, drain_outer, 0)


def local(n, n_lat, queries, key_tokens, value_tokens, block_lists, band_rows):
    tile_lat, tile_lon, feature = queries.shape
    tile = tile_lat * tile_lon
    picks = band_rows.shape[1]
    groups = feature // PAIR
    full = 5 * tile + n * picks
    vmem = pl.BlockSpec(memory_space=pltpu.VMEM)
    hbm = pl.BlockSpec(memory_space=pltpu.HBM)
    smem = pl.BlockSpec(memory_space=pltpu.SMEM)
    out = pl.pallas_call(
        functools.partial(kernel, n, n_lat, tile, picks),
        out_shape=jax.ShapeDtypeStruct((tile, feature), queries.dtype),
        in_specs=[hbm, hbm, hbm, smem, smem],
        out_specs=vmem,
        scratch_shapes=[
            pltpu.VMEM((tile, feature), queries.dtype),
            pltpu.VMEM((groups, 2, full, PAIR), jnp.bfloat16),
            pltpu.VMEM((groups, 2, picks, PAIR), jnp.bfloat16),
            pltpu.VMEM((5, picks, tile), jnp.bfloat16),
            pltpu.VMEM((2, full), jnp.float32),
            pltpu.SemaphoreType.DMA((4, groups)),
            pltpu.SemaphoreType.DMA((4, groups)),
            pltpu.SemaphoreType.DMA((n // 2,)),
            pltpu.SemaphoreType.DMA((n // 2,)),
            pltpu.SemaphoreType.DMA((4,)),
            pltpu.SemaphoreType.DMA((4,)),
            pltpu.SemaphoreType.DMA((groups,)),
            pltpu.SemaphoreType.DMA((groups,)),
            pltpu.SemaphoreType.DMA((n // 2,)),
            pltpu.SemaphoreType.DMA((n // 2,)),
            pltpu.SemaphoreType.DMA((2, groups)),
            pltpu.SemaphoreType.DMA,
        ],
        compiler_params=pltpu.CompilerParams(
            collective_id=0, has_side_effects=True, vmem_limit_bytes=53 * 1024 * 1024
        ),
    )(
        queries.reshape(tile, feature),
        key_tokens.reshape(tile, feature),
        value_tokens.reshape(tile, feature),
        block_lists,
        band_rows,
    )
    return out.reshape(tile_lat, tile_lon, feature)


def solution(mesh):
    return jax.shard_map(
        functools.partial(local, mesh.shape["lon"], mesh.shape["lat"]),
        mesh=mesh,
        in_specs=(
            P("lat", "lon", None),
            P("lat", "lon", None),
            P("lat", "lon", None),
            P("lat", "lon", None),
            P("lat", "lon"),
        ),
        out_specs=P("lat", "lon", None),
        check_vma=False,
    )
```

```python
import functools

import jax
import jax.numpy as jnp
from jax import lax
from jax.experimental import pallas as pl
from jax.experimental.pallas import tpu as pltpu
from jax.sharding import PartitionSpec as P

HD = 64
BR = 8
BW = 16
PAIR = 2 * HD
MASKED = -1e30
MESH = pl.DeviceIdType.MESH


def kernel(
    n, n_lat, tile, picks,
    q_in, k_in, v_in, lists_ref, rows_ref,
    out_ref,
    q_ref, kv, staged, selectors, bias, send_sem, recv_sem, far_send, far_recv, hot_send, hot_recv,
    outer_send, outer_recv, beyond_send, beyond_recv, load_sem, q_sem,
):
    groups = kv.shape[0]
    near = 5 * tile
    full = near + n * picks
    block = tile // 2
    half = n // 2
    early = 2
    me = lax.axis_index("lon")
    lat = lax.axis_index("lat")
    polar = (lat == 0) | (lat == n_lat - 1)
    window = jnp.where(lat == 1, 3, 4)
    odd = lax.rem(me, 2)
    partner = me + 1 - 2 * odd
    east = lax.rem(me + 2, n)
    west = lax.rem(me + n - 2, n)

    def load(g, which):
        columns = pl.ds(pl.multiple_of(g * PAIR, PAIR), PAIR)
        return pltpu.make_async_copy(
            (k_in, v_in)[which].at[:, columns],
            kv.at[g, which, pl.ds(2 * tile, tile)],
            load_sem.at[which, g],
        )

    barrier = pltpu.get_barrier_semaphore()

    def greet(peer):
        pl.semaphore_signal(barrier, inc=1, device_id={"lon": peer}, device_id_type=MESH)

    greet(partner)
    greet(east)
    greet(west)

    @pl.when(polar)
    def _():
        def greet_far(step, carry):
            greet(lax.rem(me + 2 * step, n))
            return carry

        lax.fori_loop(2, half - 1, greet_far, 0)

    for g in range(groups):
        load(g, 0).start()
        load(g, 1).start()
    q_load = pltpu.make_async_copy(q_in, q_ref, q_sem)
    q_load.start()

    def band_rows_of(j):
        place = lax.rem(j, 2) * half + j // 2
        return pl.ds(pl.multiple_of(near + place * picks, picks), picks)

    pl.semaphore_wait(barrier, jnp.where(polar, half, 3))

    def tile_rows(t):
        return pl.ds(pl.multiple_of(t * tile, tile), tile)

    def own_copy(kind, g):
        target, t = ((east, 0), (west, 4), (partner, 1 + 2 * odd))[kind]
        return pltpu.make_async_remote_copy(
            src_ref=kv.at[g, :, tile_rows(2)],
            dst_ref=kv.at[g, :, tile_rows(t)],
            send_sem=send_sem.at[kind, g],
            recv_sem=recv_sem.at[kind, g],
            device_id={"lon": target},
            device_id_type=MESH,
        )

    def relay_copy(g):
        return pltpu.make_async_remote_copy(
            src_ref=kv.at[g, :, tile_rows(4 - 4 * odd)],
            dst_ref=kv.at[g, :, tile_rows(3 - 2 * odd)],
            send_sem=send_sem.at[3, g],
            recv_sem=recv_sem.at[3, g],
            device_id={"lon": partner},
            device_id_type=MESH,
        )

    def far_copy(step):
        return pltpu.make_async_remote_copy(
            src_ref=staged,
            dst_ref=kv.at[:, :, band_rows_of(me)],
            send_sem=far_send.at[step],
            recv_sem=far_recv.at[step],
            device_id={"lon": lax.rem(me + 2 * step, n)},
            device_id_type=MESH,
        )

    def far_arrival(step):
        return pltpu.make_async_remote_copy(
            src_ref=staged,
            dst_ref=kv.at[:, :, band_rows_of(lax.rem(me + n - 2 * step, n))],
            send_sem=far_send.at[step],
            recv_sem=far_recv.at[step],
            device_id={"lon": lax.rem(me + 2 * step, n)},
            device_id_type=MESH,
        )

    def hot_copy(kind):
        target, t = ((east, 0), (west, 4), (partner, 1 + 2 * odd), (partner, 3 - 2 * odd))[kind]
        return pltpu.make_async_remote_copy(
            src_ref=selectors.at[2 if kind < 3 else 4 - 4 * odd],
            dst_ref=selectors.at[t],
            send_sem=hot_send.at[kind],
            recv_sem=hot_recv.at[kind],
            device_id={"lon": target},
            device_id_type=MESH,
        )

    def hot_arrival(kind):
        t = (0, 4, 3 - 2 * odd, 1 + 2 * odd)[kind]
        return pltpu.make_async_remote_copy(
            src_ref=selectors.at[2],
            dst_ref=selectors.at[t],
            send_sem=hot_send.at[kind],
            recv_sem=hot_recv.at[kind],
            device_id={"lon": partner},
            device_id_type=MESH,
        )

    def outer_rows(j):
        return band_rows_of(lax.rem(j + n + 4 * lax.rem(j, 2) - 2, n))

    def outer_copy(g, j):
        return pltpu.make_async_remote_copy(
            src_ref=kv.at[g, :, outer_rows(j)],
            dst_ref=kv.at[g, :, outer_rows(j)],
            send_sem=outer_send.at[g],
            recv_sem=outer_recv.at[g],
            device_id={"lon": partner},
            device_id_type=MESH,
        )

    def beyond_copy(step, j):
        rows = band_rows_of(lax.rem(j + n - 2 * step, n))
        return pltpu.make_async_remote_copy(
            src_ref=kv.at[:, :, rows],
            dst_ref=kv.at[:, :, rows],
            send_sem=beyond_send.at[step],
            recv_sem=beyond_recv.at[step],
            device_id={"lon": partner},
            device_id_type=MESH,
        )

    def pick(g, t, peer):
        for which in range(2):
            rows = kv[g, which, tile_rows(t), :]
            picked = jnp.dot(selectors[t], rows, preferred_element_type=jnp.float32)
            kv[g, which, band_rows_of(peer), :] = picked.astype(jnp.bfloat16)

    def arrival(kind, t, g):
        return pltpu.make_async_remote_copy(
            src_ref=kv.at[g, :, tile_rows(2)],
            dst_ref=kv.at[g, :, tile_rows(t)],
            send_sem=send_sem.at[0, g],
            recv_sem=recv_sem.at[kind, g],
            device_id={"lon": partner},
            device_id_type=MESH,
        )

    def send_own(g, carry):
        load(g, 0).wait()
        load(g, 1).wait()
        for kind in range(3):
            own_copy(kind, g).start()
        return carry

    lax.fori_loop(0, early, send_own, 0)

    @pl.when(polar)
    def _():
        row = lax.broadcasted_iota(jnp.int32, (picks, tile), 0)
        token = lax.broadcasted_iota(jnp.int32, (picks, tile), 1)
        hot = jnp.zeros((picks, tile), jnp.float32)
        for i in range(picks):
            hot = jnp.where((row == i) & (token == rows_ref[0, i]), 1.0, hot)
        selectors[2] = hot.astype(jnp.bfloat16)
        for kind in range(3):
            hot_copy(kind).start()

    def await_load(g, carry):
        load(g, 0).wait()
        load(g, 1).wait()
        return carry

    lax.fori_loop(early, groups, await_load, 0)

    @pl.when(polar)
    def _():
        def pick_own(g, carry):
            for which in range(2):
                rows = kv[g, which, 2 * tile:3 * tile, :]
                picked = jnp.dot(selectors[2], rows, preferred_element_type=jnp.float32)
                staged[g, which] = picked.astype(jnp.bfloat16)
                kv[g, which, band_rows_of(me), :] = picked.astype(jnp.bfloat16)
            return carry

        lax.fori_loop(0, groups, pick_own, 0)

        def send(step, carry):
            far_copy(step).start()
            return carry

        lax.fori_loop(2, half - 1, send, 0)

    def send_rest(g, carry):
        for kind in range(3):
            own_copy(kind, g).start()
        return carry

    lax.fori_loop(early, window, send_rest, 0)

    candidate = lax.broadcasted_iota(jnp.int32, (1, full), 1) // block
    for b in range(2):
        listed = candidate >= 10
        for slot in range(lists_ref.shape[2]):
            listed = listed | (candidate == lists_ref[b, 0, slot])
        bias[b:b + 1, :] = jnp.where(listed, 0.0, MASKED)

    q_load.wait()

    def relay(g):
        arrival(1 - odd, 4 - 4 * odd, g).wait_recv()
        relay_copy(g).start()
        arrival(odd, 4 * odd, g).wait_recv()

        @pl.when(polar)
        def _():
            pick(g, 0, west)
            pick(g, 4, east)
            outer_copy(g, me).start()

    def attend(g, rows):
        columns = pl.ds(pl.multiple_of(g * PAIR, PAIR), PAIR)
        q = q_ref[:, columns] * jnp.bfloat16(HD ** -0.5)
        keys = kv[g, 0, 0:rows, :]
        values = jnp.concatenate(
            [kv[g, 1, 0:rows, :], jnp.ones((rows, PAIR), jnp.bfloat16)], axis=1
        )
        first = lax.broadcasted_iota(jnp.int32, (tile, PAIR), 1) < HD
        results = []
        for head in range(2):
            mine = first if head == 0 else ~first
            q_head = jnp.where(mine, q, jnp.zeros_like(q))
            scores = lax.dot_general(
                q_head, keys, (((1,), (1,)), ((), ())), preferred_element_type=jnp.float32
            )
            scores = scores.reshape(2, block, rows) + bias[:, 0:rows][:, None, :]
            scores = scores.reshape(tile, rows)
            row_max = jnp.max(scores, axis=-1, keepdims=True)
            weights = jnp.exp(scores - row_max).astype(jnp.bfloat16)
            mixed = jnp.dot(weights, values, preferred_element_type=jnp.float32)
            results.append(mixed[:, :PAIR] / mixed[:, PAIR:])
        out_ref[:, columns] = jnp.where(first, results[0], results[1]).astype(out_ref.dtype)

    @pl.when(polar)
    def _():
        for kind in range(2):
            hot_arrival(kind).wait_recv()
        hot_copy(3).start()

        def take(s, c):
            far_arrival(s).wait_recv()
            beyond_copy(s, me).start()
            return c

        lax.fori_loop(2, half - 1, take, 0)

    relay(0)

    def step(g, carry):
        @pl.when(g + 1 < groups)
        def _():
            relay(g + 1)

        @pl.when(g + window < groups)
        def _():
            for kind in range(3):
                own_copy(kind, g).wait_send()
            for kind in range(3):
                own_copy(kind, g + window).start()

        arrival(2, 3 - 2 * odd, g).wait_recv()
        arrival(3, 1 + 2 * odd, g).wait_recv()

        @pl.when(polar)
        def _():
            @pl.when(g == 0)
            def _():
                hot_arrival(2).wait_recv()
                hot_arrival(3).wait_recv()

                def take_beyond(s, c):
                    beyond_copy(s, partner).wait_recv()
                    return c

                lax.fori_loop(2, half - 1, take_beyond, 0)

            pick(g, 3 - 2 * odd, partner)
            pick(g, 1 + 2 * odd, lax.rem(me + n - 1 + 2 * odd, n))
            outer_copy(g, partner).wait_recv()
            attend(g, full)

        @pl.when(jnp.logical_not(polar))
        def _():
            attend(g, near)

        return carry

    lax.fori_loop(0, groups, step, 0)

    def drain(g, carry):
        @pl.when(g + window >= groups)
        def _():
            for kind in range(3):
                own_copy(kind, g).wait_send()

        relay_copy(g).wait_send()
        return carry

    lax.fori_loop(0, groups, drain, 0)

    @pl.when(polar)
    def _():
        for kind in range(4):
            hot_copy(kind).wait_send()

        def drain_far(s, c):
            far_copy(s).wait_send()
            beyond_copy(s, me).wait_send()
            return c

        lax.fori_loop(2, half - 1, drain_far, 0)

        def drain_outer(g, c):
            outer_copy(g, me).wait_send()
            return c

        lax.fori_loop(0, groups, drain_outer, 0)


def local(n, n_lat, queries, key_tokens, value_tokens, block_lists, band_rows):
    tile_lat, tile_lon, feature = queries.shape
    tile = tile_lat * tile_lon
    picks = band_rows.shape[1]
    groups = feature // PAIR
    full = 5 * tile + n * picks
    vmem = pl.BlockSpec(memory_space=pltpu.VMEM)
    hbm = pl.BlockSpec(memory_space=pltpu.HBM)
    smem = pl.BlockSpec(memory_space=pltpu.SMEM)
    out = pl.pallas_call(
        functools.partial(kernel, n, n_lat, tile, picks),
        out_shape=jax.ShapeDtypeStruct((tile, feature), queries.dtype),
        in_specs=[hbm, hbm, hbm, smem, smem],
        out_specs=vmem,
        scratch_shapes=[
            pltpu.VMEM((tile, feature), queries.dtype),
            pltpu.VMEM((groups, 2, full, PAIR), jnp.bfloat16),
            pltpu.VMEM((groups, 2, picks, PAIR), jnp.bfloat16),
            pltpu.VMEM((5, picks, tile), jnp.bfloat16),
            pltpu.VMEM((2, full), jnp.float32),
            pltpu.SemaphoreType.DMA((4, groups)),
            pltpu.SemaphoreType.DMA((4, groups)),
            pltpu.SemaphoreType.DMA((n // 2,)),
            pltpu.SemaphoreType.DMA((n // 2,)),
            pltpu.SemaphoreType.DMA((4,)),
            pltpu.SemaphoreType.DMA((4,)),
            pltpu.SemaphoreType.DMA((groups,)),
            pltpu.SemaphoreType.DMA((groups,)),
            pltpu.SemaphoreType.DMA((n // 2,)),
            pltpu.SemaphoreType.DMA((n // 2,)),
            pltpu.SemaphoreType.DMA((2, groups)),
            pltpu.SemaphoreType.DMA,
        ],
        compiler_params=pltpu.CompilerParams(
            collective_id=0, has_side_effects=True, vmem_limit_bytes=53 * 1024 * 1024
        ),
    )(
        queries.reshape(tile, feature),
        key_tokens.reshape(tile, feature),
        value_tokens.reshape(tile, feature),
        block_lists,
        band_rows,
    )
    return out.reshape(tile_lat, tile_lon, feature)


def solution(mesh):
    return jax.shard_map(
        functools.partial(local, mesh.shape["lon"], mesh.shape["lat"]),
        mesh=mesh,
        in_specs=(
            P("lat", "lon", None),
            P("lat", "lon", None),
            P("lat", "lon", None),
            P("lat", "lon", None),
            P("lat", "lon"),
        ),
        out_specs=P("lat", "lon", None),
        check_vma=False,
    )
```

```python
import functools

import jax
import jax.numpy as jnp
from jax import lax
from jax.experimental import pallas as pl
from jax.experimental.pallas import tpu as pltpu
from jax.sharding import PartitionSpec as P

HD = 64
BR = 8
BW = 16
PAIR = 2 * HD
MASKED = -1e30
MESH = pl.DeviceIdType.MESH


def kernel(
    n, n_lat, tile, picks,
    q_in, k_in, v_in, lists_ref, rows_ref,
    out_ref,
    q_ref, kv, staged, selectors, bias, send_sem, recv_sem, far_send, far_recv, hot_send, hot_recv,
    outer_send, outer_recv, beyond_send, beyond_recv, load_sem, q_sem,
):
    groups = kv.shape[0]
    near = 5 * tile
    full = near + n * picks
    block = tile // 2
    half = n // 2
    early = 2
    window = 6
    me = lax.axis_index("lon")
    lat = lax.axis_index("lat")
    polar = (lat == 0) | (lat == n_lat - 1)
    odd = lax.rem(me, 2)
    partner = me + 1 - 2 * odd
    east = lax.rem(me + 2, n)
    west = lax.rem(me + n - 2, n)

    def load(g, which):
        columns = pl.ds(pl.multiple_of(g * PAIR, PAIR), PAIR)
        return pltpu.make_async_copy(
            (k_in, v_in)[which].at[:, columns],
            kv.at[g, which, pl.ds(2 * tile, tile)],
            load_sem.at[which, g],
        )

    barrier = pltpu.get_barrier_semaphore()

    def greet(peer):
        pl.semaphore_signal(barrier, inc=1, device_id={"lon": peer}, device_id_type=MESH)

    greet(partner)
    greet(east)
    greet(west)

    @pl.when(polar)
    def _():
        def greet_far(step, carry):
            greet(lax.rem(me + 2 * step, n))
            return carry

        lax.fori_loop(2, half - 1, greet_far, 0)

    for g in range(groups):
        load(g, 0).start()
        load(g, 1).start()
    q_load = pltpu.make_async_copy(q_in, q_ref, q_sem)
    q_load.start()

    def band_rows_of(j):
        place = lax.rem(j, 2) * half + j // 2
        return pl.ds(pl.multiple_of(near + place * picks, picks), picks)

    pl.semaphore_wait(barrier, jnp.where(polar, half, 3))

    def tile_rows(t):
        return pl.ds(pl.multiple_of(t * tile, tile), tile)

    def own_copy(kind, g):
        target, t = ((east, 0), (west, 4), (partner, 1 + 2 * odd))[kind]
        return pltpu.make_async_remote_copy(
            src_ref=kv.at[g, :, tile_rows(2)],
            dst_ref=kv.at[g, :, tile_rows(t)],
            send_sem=send_sem.at[kind, g],
            recv_sem=recv_sem.at[kind, g],
            device_id={"lon": target},
            device_id_type=MESH,
        )

    def relay_copy(g):
        return pltpu.make_async_remote_copy(
            src_ref=kv.at[g, :, tile_rows(4 - 4 * odd)],
            dst_ref=kv.at[g, :, tile_rows(3 - 2 * odd)],
            send_sem=send_sem.at[3, g],
            recv_sem=recv_sem.at[3, g],
            device_id={"lon": partner},
            device_id_type=MESH,
        )

    def far_copy(step):
        return pltpu.make_async_remote_copy(
            src_ref=staged,
            dst_ref=kv.at[:, :, band_rows_of(me)],
            send_sem=far_send.at[step],
            recv_sem=far_recv.at[step],
            device_id={"lon": lax.rem(me + 2 * step, n)},
            device_id_type=MESH,
        )

    def far_arrival(step):
        return pltpu.make_async_remote_copy(
            src_ref=staged,
            dst_ref=kv.at[:, :, band_rows_of(lax.rem(me + n - 2 * step, n))],
            send_sem=far_send.at[step],
            recv_sem=far_recv.at[step],
            device_id={"lon": lax.rem(me + 2 * step, n)},
            device_id_type=MESH,
        )

    def hot_copy(kind):
        target, t = ((east, 0), (west, 4), (partner, 1 + 2 * odd), (partner, 3 - 2 * odd))[kind]
        return pltpu.make_async_remote_copy(
            src_ref=selectors.at[2 if kind < 3 else 4 - 4 * odd],
            dst_ref=selectors.at[t],
            send_sem=hot_send.at[kind],
            recv_sem=hot_recv.at[kind],
            device_id={"lon": target},
            device_id_type=MESH,
        )

    def hot_arrival(kind):
        t = (0, 4, 3 - 2 * odd, 1 + 2 * odd)[kind]
        return pltpu.make_async_remote_copy(
            src_ref=selectors.at[2],
            dst_ref=selectors.at[t],
            send_sem=hot_send.at[kind],
            recv_sem=hot_recv.at[kind],
            device_id={"lon": partner},
            device_id_type=MESH,
        )

    def outer_rows(j):
        return band_rows_of(lax.rem(j + n + 4 * lax.rem(j, 2) - 2, n))

    def outer_copy(g, j):
        return pltpu.make_async_remote_copy(
            src_ref=kv.at[g, :, outer_rows(j)],
            dst_ref=kv.at[g, :, outer_rows(j)],
            send_sem=outer_send.at[g],
            recv_sem=outer_recv.at[g],
            device_id={"lon": partner},
            device_id_type=MESH,
        )

    def beyond_copy(step, j):
        rows = band_rows_of(lax.rem(j + n - 2 * step, n))
        return pltpu.make_async_remote_copy(
            src_ref=kv.at[:, :, rows],
            dst_ref=kv.at[:, :, rows],
            send_sem=beyond_send.at[step],
            recv_sem=beyond_recv.at[step],
            device_id={"lon": partner},
            device_id_type=MESH,
        )

    def pick(g, t, peer):
        for which in range(2):
            rows = kv[g, which, tile_rows(t), :]
            picked = jnp.dot(selectors[t], rows, preferred_element_type=jnp.float32)
            kv[g, which, band_rows_of(peer), :] = picked.astype(jnp.bfloat16)

    def arrival(kind, t, g):
        return pltpu.make_async_remote_copy(
            src_ref=kv.at[g, :, tile_rows(2)],
            dst_ref=kv.at[g, :, tile_rows(t)],
            send_sem=send_sem.at[0, g],
            recv_sem=recv_sem.at[kind, g],
            device_id={"lon": partner},
            device_id_type=MESH,
        )

    def send_own(g, carry):
        load(g, 0).wait()
        load(g, 1).wait()
        for kind in range(3):
            own_copy(kind, g).start()
        return carry

    lax.fori_loop(0, early, send_own, 0)

    @pl.when(polar)
    def _():
        row = lax.broadcasted_iota(jnp.int32, (picks, tile), 0)
        token = lax.broadcasted_iota(jnp.int32, (picks, tile), 1)
        hot = jnp.zeros((picks, tile), jnp.float32)
        for i in range(picks):
            hot = jnp.where((row == i) & (token == rows_ref[0, i]), 1.0, hot)
        selectors[2] = hot.astype(jnp.bfloat16)
        for kind in range(3):
            hot_copy(kind).start()

    def await_load(g, carry):
        load(g, 0).wait()
        load(g, 1).wait()
        return carry

    lax.fori_loop(early, groups, await_load, 0)

    @pl.when(polar)
    def _():
        def pick_own(g, carry):
            for which in range(2):
                rows = kv[g, which, 2 * tile:3 * tile, :]
                picked = jnp.dot(selectors[2], rows, preferred_element_type=jnp.float32)
                staged[g, which] = picked.astype(jnp.bfloat16)
                kv[g, which, band_rows_of(me), :] = picked.astype(jnp.bfloat16)
            return carry

        lax.fori_loop(0, groups, pick_own, 0)

        def send(step, carry):
            far_copy(step).start()
            return carry

        lax.fori_loop(2, half - 1, send, 0)

    def send_rest(g, carry):
        for kind in range(3):
            own_copy(kind, g).start()
        return carry

    lax.fori_loop(early, window, send_rest, 0)

    candidate = lax.broadcasted_iota(jnp.int32, (1, full), 1) // block
    for b in range(2):
        listed = candidate >= 10
        for slot in range(lists_ref.shape[2]):
            listed = listed | (candidate == lists_ref[b, 0, slot])
        bias[b:b + 1, :] = jnp.where(listed, 0.0, MASKED)

    q_load.wait()

    def relay(g):
        arrival(1 - odd, 4 - 4 * odd, g).wait_recv()
        relay_copy(g).start()

        @pl.when(polar)
        def _():
            arrival(odd, 4 * odd, g).wait_recv()
            pick(g, 0, west)
            pick(g, 4, east)
            outer_copy(g, me).start()

    def attend(g, rows):
        columns = pl.ds(pl.multiple_of(g * PAIR, PAIR), PAIR)
        q = q_ref[:, columns] * jnp.bfloat16(HD ** -0.5)
        keys = kv[g, 0, 0:rows, :]
        values = jnp.concatenate(
            [kv[g, 1, 0:rows, :], jnp.ones((rows, PAIR), jnp.bfloat16)], axis=1
        )
        first = lax.broadcasted_iota(jnp.int32, (tile, PAIR), 1) < HD
        results = []
        for head in range(2):
            mine = first if head == 0 else ~first
            q_head = jnp.where(mine, q, jnp.zeros_like(q))
            scores = lax.dot_general(
                q_head, keys, (((1,), (1,)), ((), ())), preferred_element_type=jnp.float32
            )
            scores = scores.reshape(2, block, rows) + bias[:, 0:rows][:, None, :]
            scores = scores.reshape(tile, rows)
            row_max = jnp.max(scores, axis=-1, keepdims=True)
            weights = jnp.exp(scores - row_max).astype(jnp.bfloat16)
            mixed = jnp.dot(weights, values, preferred_element_type=jnp.float32)
            results.append(mixed[:, :PAIR] / mixed[:, PAIR:])
        out_ref[:, columns] = jnp.where(first, results[0], results[1]).astype(out_ref.dtype)

    @pl.when(polar)
    def _():
        for kind in range(2):
            hot_arrival(kind).wait_recv()
        hot_copy(3).start()

        def take(s, c):
            far_arrival(s).wait_recv()
            beyond_copy(s, me).start()
            return c

        lax.fori_loop(2, half - 1, take, 0)

    relay(0)

    def step(g, carry):
        @pl.when(g + 1 < groups)
        def _():
            relay(g + 1)

        @pl.when(g + window < groups)
        def _():
            for kind in range(3):
                own_copy(kind, g).wait_send()
            for kind in range(3):
                own_copy(kind, g + window).start()

        arrival(2, 3 - 2 * odd, g).wait_recv()
        arrival(3, 1 + 2 * odd, g).wait_recv()

        @pl.when(polar)
        def _():
            @pl.when(g == 0)
            def _():
                hot_arrival(2).wait_recv()
                hot_arrival(3).wait_recv()

                def take_beyond(s, c):
                    beyond_copy(s, partner).wait_recv()
                    return c

                lax.fori_loop(2, half - 1, take_beyond, 0)

            pick(g, 3 - 2 * odd, partner)
            pick(g, 1 + 2 * odd, lax.rem(me + n - 1 + 2 * odd, n))
            outer_copy(g, partner).wait_recv()
            attend(g, full)

        @pl.when(jnp.logical_not(polar))
        def _():
            arrival(odd, 4 * odd, g).wait_recv()
            attend(g, near)

        return carry

    lax.fori_loop(0, groups, step, 0)

    def drain(g, carry):
        @pl.when(g + window >= groups)
        def _():
            for kind in range(3):
                own_copy(kind, g).wait_send()

        relay_copy(g).wait_send()
        return carry

    lax.fori_loop(0, groups, drain, 0)

    @pl.when(polar)
    def _():
        for kind in range(4):
            hot_copy(kind).wait_send()

        def drain_far(s, c):
            far_copy(s).wait_send()
            beyond_copy(s, me).wait_send()
            return c

        lax.fori_loop(2, half - 1, drain_far, 0)

        def drain_outer(g, c):
            outer_copy(g, me).wait_send()
            return c

        lax.fori_loop(0, groups, drain_outer, 0)


def local(n, n_lat, queries, key_tokens, value_tokens, block_lists, band_rows):
    tile_lat, tile_lon, feature = queries.shape
    tile = tile_lat * tile_lon
    picks = band_rows.shape[1]
    groups = feature // PAIR
    full = 5 * tile + n * picks
    vmem = pl.BlockSpec(memory_space=pltpu.VMEM)
    hbm = pl.BlockSpec(memory_space=pltpu.HBM)
    smem = pl.BlockSpec(memory_space=pltpu.SMEM)
    out = pl.pallas_call(
        functools.partial(kernel, n, n_lat, tile, picks),
        out_shape=jax.ShapeDtypeStruct((tile, feature), queries.dtype),
        in_specs=[hbm, hbm, hbm, smem, smem],
        out_specs=vmem,
        scratch_shapes=[
            pltpu.VMEM((tile, feature), queries.dtype),
            pltpu.VMEM((groups, 2, full, PAIR), jnp.bfloat16),
            pltpu.VMEM((groups, 2, picks, PAIR), jnp.bfloat16),
            pltpu.VMEM((5, picks, tile), jnp.bfloat16),
            pltpu.VMEM((2, full), jnp.float32),
            pltpu.SemaphoreType.DMA((4, groups)),
            pltpu.SemaphoreType.DMA((4, groups)),
            pltpu.SemaphoreType.DMA((n // 2,)),
            pltpu.SemaphoreType.DMA((n // 2,)),
            pltpu.SemaphoreType.DMA((4,)),
            pltpu.SemaphoreType.DMA((4,)),
            pltpu.SemaphoreType.DMA((groups,)),
            pltpu.SemaphoreType.DMA((groups,)),
            pltpu.SemaphoreType.DMA((n // 2,)),
            pltpu.SemaphoreType.DMA((n // 2,)),
            pltpu.SemaphoreType.DMA((2, groups)),
            pltpu.SemaphoreType.DMA,
        ],
        compiler_params=pltpu.CompilerParams(
            collective_id=0, has_side_effects=True, vmem_limit_bytes=53 * 1024 * 1024
        ),
    )(
        queries.reshape(tile, feature),
        key_tokens.reshape(tile, feature),
        value_tokens.reshape(tile, feature),
        block_lists,
        band_rows,
    )
    return out.reshape(tile_lat, tile_lon, feature)


def solution(mesh):
    return jax.shard_map(
        functools.partial(local, mesh.shape["lon"], mesh.shape["lat"]),
        mesh=mesh,
        in_specs=(
            P("lat", "lon", None),
            P("lat", "lon", None),
            P("lat", "lon", None),
            P("lat", "lon", None),
            P("lat", "lon"),
        ),
        out_specs=P("lat", "lon", None),
        check_vma=False,
    )
```
